32 devices in a mesh: gen: 8 (over z, y), grp: 4 (over x, core).
Axes of the slice: x: 2, y: 2, z: 4, core: 2. Of those that a mesh axis runs over, the one named last changes fastest.
Arguments:
- query_in: bfloat16 [4, 1024, 4096], P('grp', 'gen'), may hold values from -8 to 8, as said below
- key_in: bfloat16 [4, 1024, 4096], P('grp', 'gen'), may hold values from -8 to 8
- value_in: bfloat16 [4, 1024, 4096], P('grp', 'gen'), may hold values from -6 to 6
- teacher_w: bfloat16 [4096, 5120], P('gen'), may hold values from -0.09375 to 0.09375
- disc_heads: float32 [8, 5120], replicated, may hold values from -0.078125 to 0.078125
- frame_of_token: int32 [4, 1024], P('grp'), may hold values from 0 to 20, never falling along the last dimension, each value on 1 to 97 neighbouring positions
- head_of_frame: int32 [4, 21], P('grp'), may hold values from 0 to 7
- timestep: int32 [4], P('grp'), may hold values from 0 to 999
Outputs:
- latents: bfloat16 [4, 1024, 4096], P('grp', 'gen')
- grad_query: bfloat16 [4, 1024, 4096], P('grp', 'gen')
- grad_key: bfloat16 [4, 1024, 4096], P('grp', 'gen')
- grad_value: bfloat16 [4, 1024, 4096], P('grp', 'gen')
- grad_heads: float32 [8, 5120], replicated
The draws below stay inside these ranges and needn't reach their ends.
Inputs may be any that keep to these rules, and one draw needn't show every extreme that they name: `query_in`: entries lie within the range; in some draws a few queries equal some keys. `frame_of_token`: within a clip the frame numbers never fall along the tokens; every frame holds 1 to 97 tokens and some frame exactly 97.
All inputs are finite; a program needn't handle non-finite values.
Results may differ from the reference program's by a relative error of at most 0.035.
Values may be sent and summed in bfloat16 or wider, within the bound.
No kernel may reach another device: no remote copies, remote signals or barrier semaphores. Data moves between devices by JAX's collectives and lax.ppermute only.
A program may use at most 64 MiB of HBM per device.

```python
import math
import jax
import jax.numpy as jnp
import numpy as np
from jax import lax

HEADS = 32
HS = 128
DH = 5120
FRAMES = 21
NDH = 8
NSTEPS = 1000
TOKENS = 1024
CLIPS = 4
WIDTH = 4096
FRAME_MOST = 97


def base_values(key, salt):
    draw_key = jax.random.fold_in(key, salt)
    values = jnp.clip(jax.random.normal(draw_key, (CLIPS, TOKENS, HEADS * HS), jnp.float32), -6.0, 6.0)
    return values


def draw_query_in(key, part):
    values = base_values(key, 3)
    return values.astype(jnp.bfloat16)


def draw_key_in(key, part):
    values = base_values(key, 5)
    return values.astype(jnp.bfloat16)


def set_ends(drawn, stream_key, smallest, top_value):
    longest = drawn.shape.index(max(drawn.shape))
    spots = []
    for shift in (0, 1):
        where = [jax.random.randint(jax.random.fold_in(stream_key, axis), (), 0, length) for axis, length in enumerate(drawn.shape)]
        where[longest] = (where[longest] + shift) % drawn.shape[longest]
        spots.append(tuple(where))
    return drawn.at[spots[0]].set(smallest).at[spots[1]].set(top_value)


def shard_levels(rng, dims, cuts, low, largest):
    level = 1.0
    for dim, parts in cuts:
        steps = jax.random.uniform(jax.random.fold_in(jax.random.fold_in(rng, 6), dim), (parts,), jnp.float32, low / len(cuts), largest / len(cuts))
        level = level * jnp.repeat(jnp.exp(steps), dims[dim] // parts).reshape((-1,) + (1,) * (len(dims) - 1 - dim))
    return level


def split_up(amount, total, most, slope):
    portions = [(1 << 20) // math.isqrt(rank ** slope) + 1 for rank in range(2, amount + 1)]
    spare, holding = total - most - (amount - 1), [1] * (amount - 1)
    while spare > 0:
        candidates = [i for i in range(amount - 1) if holding[i] < most]
        mass, budget = sum([portions[i] for i in candidates]), spare
        for i in candidates:
            addition = min(most - holding[i], max(1, budget * portions[i] // mass), spare)
            holding[i] = holding[i] + addition
            spare = spare - addition
    return np.array([most] + holding)


def ragged(stream_key, number_of, total, limit, skew):
    if number_of == 2:
        one = jax.random.randint(stream_key, (), max(1, total - limit), min(limit, total - 1) + 1)
        return jnp.stack([one, total - one])
    tallies = jnp.asarray(split_up(number_of, total, limit, skew), jnp.int32)
    couples = (number_of - 1) // 2
    giver, sink = tallies[1:1 + 2 * couples:2], tallies[2:2 + 2 * couples:2]
    slack = jnp.minimum(giver - 1, limit - sink)
    passed = jax.random.randint(jax.random.fold_in(stream_key, 1), (couples,), 0, 1 << 20) % (slack + 1)
    tallies = tallies.at[1:1 + 2 * couples:2].set(giver - passed).at[2:2 + 2 * couples:2].set(sink + passed)
    return tallies[jax.random.permutation(jax.random.fold_in(stream_key, 2), number_of)]


def scatter_about(own_key, shape, scale, most, cuts=(), kind=jnp.bfloat16):
    values = scale * jax.random.normal(own_key, shape, jnp.float32)
    if cuts:
        values = values * shard_levels(own_key, shape, cuts, -0.22, 0.18)
    return jnp.clip(values, -most, most).astype(kind)


def setup_inputs(seed: int = 0) -> dict:
    key_list = jax.random.split(jax.random.key(seed), 9)
    return {
        "query_in": draw_query_in(jax.random.fold_in(key_list[8], 71), 0),
        "key_in": draw_key_in(jax.random.fold_in(key_list[8], 71), 0),
        "value_in": scatter_about(key_list[2], (CLIPS, TOKENS, WIDTH), 1.0, 6.0, ((0, 4), (1, 8))),
        "teacher_w": scatter_about(key_list[3], (WIDTH, DH), WIDTH ** -0.5, 0.09375, ((0, 8),)),
        "disc_heads": scatter_about(key_list[4], (NDH, DH), DH ** -0.5, 0.078125, (), jnp.float32),
        "frame_of_token": jax.vmap(lambda own: jnp.searchsorted(jnp.cumsum(ragged(own, FRAMES, TOKENS, FRAME_MOST, 1)), jnp.arange(TOKENS), side="right"))(jax.random.split(key_list[5], CLIPS)).reshape((CLIPS, TOKENS)).astype(jnp.int32),
        "head_of_frame": set_ends(jax.random.randint(key_list[6], (CLIPS, FRAMES), 0, NDH), jax.random.fold_in(key_list[6], 1), 0, NDH - 1).astype(jnp.int32),
        "timestep": set_ends(jax.random.randint(key_list[7], (CLIPS,), 0, NSTEPS), jax.random.fold_in(key_list[7], 1), 0, NSTEPS - 1).astype(jnp.int32),
    }


epsilon = 1e-06

def attend(items):
    head_query, head_key, head_value = items
    inv_scale = 1.0 / math.sqrt(HS)
    scores = jnp.dot(head_query, head_key.T, preferred_element_type=jnp.float32) * inv_scale
    peak = lax.optimization_barrier(jnp.max(scores, axis=1, keepdims=True))
    weights = jnp.exp(scores - peak)
    total = lax.optimization_barrier(jnp.sum(weights, axis=1, keepdims=True))
    mixed = jnp.dot(weights.astype(jnp.bfloat16), head_value, preferred_element_type=jnp.float32) / total
    return (mixed.astype(jnp.bfloat16), (peak + jnp.log(total))[:, 0])

def attend_back(items):
    head_query, head_key, head_value, lse_rows, grad_rows, delta_rows = items
    inv_scale = 1.0 / math.sqrt(HS)
    scores = jnp.dot(head_query, head_key.T, preferred_element_type=jnp.float32) * inv_scale
    probs = jnp.exp(scores - lse_rows[:, None])
    grad_value = jnp.dot(probs.astype(jnp.bfloat16).T, grad_rows, preferred_element_type=jnp.float32)
    grad_probs = jnp.dot(grad_rows, head_value.T, preferred_element_type=jnp.float32)
    dscore = (probs * (grad_probs - delta_rows[:, None]) * inv_scale).astype(jnp.bfloat16)
    grad_query = jnp.dot(dscore, head_key, preferred_element_type=jnp.float32)
    grad_key = jnp.dot(dscore.T, head_query, preferred_element_type=jnp.float32)
    return (grad_query.astype(jnp.bfloat16), grad_key.astype(jnp.bfloat16), grad_value.astype(jnp.bfloat16))

def split_heads(array):
    return array.reshape(TOKENS, HEADS, HS).transpose(1, 0, 2)

def join_heads(array):
    return array.transpose(1, 0, 2).reshape(TOKENS, WIDTH)

def one_clip(items, teacher_w, disc_heads):
    query_clip, key_clip, value_clip, frames, head_index, tstep = items
    head_query = split_heads(query_clip)
    head_key = split_heads(key_clip)
    head_value = split_heads(value_clip)
    mixed, lse = lax.map(attend, (head_query, head_key, head_value))
    latent = join_heads(mixed)
    member = frames[None, :] == jnp.arange(FRAMES, dtype=jnp.int32)[:, None]
    counts = lax.optimization_barrier(jnp.sum(member.astype(jnp.float32), axis=1))
    pooled = jnp.dot(member.astype(jnp.bfloat16), latent, preferred_element_type=jnp.float32) / counts[:, None]
    squares = lax.optimization_barrier(jnp.sum(pooled * pooled, axis=1))
    projected = jnp.dot(pooled.astype(jnp.bfloat16), teacher_w, preferred_element_type=jnp.float32)
    root = jnp.sqrt(squares / WIDTH + epsilon)
    pre = projected / root[:, None]
    gate = jax.nn.sigmoid(pre)
    feature = pre * gate
    picked = (head_index[:, None] == jnp.arange(NDH, dtype=jnp.int32)[None, :]).astype(jnp.float32)
    head_rows = jnp.dot(picked, disc_heads, precision=lax.Precision.HIGHEST)
    score = lax.optimization_barrier(jnp.sum(feature * head_rows, axis=1))
    weight = (tstep.astype(jnp.float32) + 1.0) / NSTEPS
    grad_score = -weight * jax.nn.sigmoid(-score) / FRAMES
    grad_heads = jnp.dot(picked.T, grad_score[:, None] * feature, precision=lax.Precision.HIGHEST)
    grad_pre = grad_score[:, None] * head_rows * gate * (1.0 + pre * (1.0 - gate))
    grad_projected = (grad_pre / root[:, None]).astype(jnp.bfloat16)
    grad_root = -lax.optimization_barrier(jnp.sum(grad_pre * pre, axis=1)) / root
    grad_pooled = jnp.dot(grad_projected, teacher_w.T, preferred_element_type=jnp.float32) + (grad_root / root / WIDTH)[:, None] * pooled
    spread = grad_pooled / counts[:, None]
    grad_latent = (TOKENS * jnp.take(spread, frames, axis=0)).astype(jnp.bfloat16)
    product = grad_latent.astype(jnp.float32) * latent.astype(jnp.float32)
    delta = lax.optimization_barrier(jnp.sum(product.reshape(TOKENS, HEADS, HS), axis=2)).T
    grad_q, grad_k, grad_v = lax.map(attend_back, (head_query, head_key, head_value, lse, split_heads(grad_latent), delta))
    return (latent, join_heads(grad_q), join_heads(grad_k), join_heads(grad_v), grad_heads)

def reference(query_in, key_in, value_in, teacher_w, disc_heads, frame_of_token, head_of_frame, timestep):

    def clip_fn(items):
        return one_clip(items, teacher_w, disc_heads)
    latents, grad_query, grad_key, grad_value, head_terms = lax.map(clip_fn, (query_in, key_in, value_in, frame_of_token, head_of_frame, timestep))
    return (latents, grad_query, grad_key, grad_value, lax.optimization_barrier(jnp.sum(head_terms, axis=0)))
```

```python
import functools
import math

import jax
import jax.numpy as jnp
from jax import lax
from jax.experimental import pallas as pl
from jax.experimental.pallas import tpu as pltpu
from jax.sharding import PartitionSpec as P

HS = 128
FRAMES = 21
FR = 24
NDH = 8
NSTEPS = 1000
LANES = 128
epsilon = 1e-06
SCALE = 1.0 / math.sqrt(HS)
LOG2E = math.log2(math.e)
BF = jnp.bfloat16
F32 = jnp.float32
VMEM_LIMIT = 48 * 1024 * 1024


def params(axes=1):
    return pltpu.CompilerParams(
        vmem_limit_bytes=VMEM_LIMIT, dimension_semantics=("arbitrary",) * axes
    )


def dot_nn(a, b):
    return lax.dot_general(a, b, (((1,), (0,)), ((), ())), preferred_element_type=F32)


def dot_nt(a, b):
    return lax.dot_general(a, b, (((1,), (1,)), ((), ())), preferred_element_type=F32)


def dot_tn(a, b):
    return lax.dot_general(a, b, (((0,), (0,)), ((), ())), preferred_element_type=F32)


def rows_of(ref):
    block = ref[...]
    return block.reshape(block.shape[-3] * block.shape[-2], block.shape[-1])


def split_three(value):
    high = value.astype(BF)
    rest = value - high.astype(F32)
    middle = rest.astype(BF)
    low = (rest - middle.astype(F32)).astype(BF)
    return high, middle, low


def lanes_three(value, shape, first):
    lane = lax.broadcasted_iota(jnp.int32, shape, 1)
    out = jnp.zeros(shape, F32)
    for i, part in enumerate(split_three(value)):
        out = jnp.where(lane == first + i, part.astype(F32), out)
    return out


def ones_three(shape):
    lane = lax.broadcasted_iota(jnp.int32, shape, 1)
    return jnp.where(lane < 3, 1.0, 0.0).astype(BF)


def take_lanes(block, first, count):
    lane = lax.broadcasted_iota(jnp.int32, block.shape, 1)
    keep = (lane >= first) & (lane < first + count)
    return jnp.sum(jnp.where(keep, block, 0.0), axis=1, keepdims=True)


def row_chunk(tokens):
    return min(256, tokens)


def stats_kernel(q_ref, k_ref, mt_ref, aug_ref, r_ref):
    blocks = q_ref.shape[0]
    tokens = blocks * LANES
    chunk = row_chunk(tokens)
    per = chunk // LANES
    keys = rows_of(k_ref)

    def step(i, total_r):
        q = q_ref[pl.ds(i * per, per)].reshape(chunk, HS)
        s = dot_nt(q, keys) * (SCALE * LOG2E)
        peak = jnp.max(s, axis=1, keepdims=True)
        e = jnp.exp2(s - peak)
        total = jnp.sum(e, axis=1, keepdims=True)
        p = (e * (1.0 / total)).astype(BF)
        lse = (peak + jnp.log2(total)) * (-1.0 / (SCALE * LOG2E))
        aug_ref[0, pl.ds(pl.multiple_of(i * chunk, chunk), chunk)] = lanes_three(
            lse, (chunk, LANES), 0
        ).astype(BF)
        return total_r + dot_nn(mt_ref[i], p)

    zero = jnp.zeros((FR, tokens), F32)
    r = run_steps(tokens // chunk, step, zero)
    for d in range(blocks):
        r_ref[d, 0] = r[:, d * LANES : (d + 1) * LANES].astype(BF)


def run_steps(count, step, carry):
    if count <= 4:
        for i in range(count):
            carry = step(i, carry)
        return carry
    return lax.fori_loop(0, count, step, carry)


def pool_kernel(blocks, heads, chunk, r_ref, v_ref, meta_ref, w_ref, part_ref, pooled_ref):
    count = jnp.maximum(take_lanes(meta_ref[...], 0, 1), 1.0)
    columns = []
    for h in range(heads):
        r = jnp.concatenate([r_ref[d, h] for d in range(blocks)], axis=1)
        v = jnp.concatenate(
            [v_ref[d, :, h * HS : (h + 1) * HS] for d in range(blocks)], axis=0
        )
        columns.append(dot_nn(r, v))
    pooled = jnp.concatenate(columns, axis=1) if heads > 1 else columns[0]
    pooled = pooled / count
    pooled_ref[...] = pooled
    squares = jnp.sum(pooled * pooled, axis=1, keepdims=True)
    stats = lanes_three(squares, (FR, LANES), 0).astype(BF)
    rounded = pooled.astype(BF)
    for d in range(blocks):
        w = w_chunk(w_ref, d, chunk)
        part_ref[d, :, :chunk] = dot_nn(rounded, w).astype(BF)
        part_ref[d, :, chunk:] = stats


def w_chunk(w_ref, d, chunk):
    if len(w_ref.shape) == 3:
        return w_ref[d]
    return w_ref[:, d * chunk : (d + 1) * chunk]


def middle_kernel(blocks, chunk, width, got_ref, rows_ref, send_ref, feature_ref, root_ref):
    total = got_ref[0].astype(F32)
    for d in range(1, blocks):
        total = total + got_ref[d].astype(F32)
    projected = total[:, :chunk]
    squares = take_lanes(total[:, chunk:], 0, 3)
    root = jnp.sqrt(squares / width + epsilon)
    pre = projected / root
    gate = jax.nn.sigmoid(pre)
    feature = pre * gate
    head_rows = rows_ref[...]
    direction = head_rows * gate * (1.0 + pre * (1.0 - gate))
    score = jnp.sum(feature * head_rows, axis=1, keepdims=True)
    slope = jnp.sum(direction * pre, axis=1, keepdims=True)
    stats = (
        lanes_three(score, (FR, LANES), 0) + lanes_three(slope, (FR, LANES), 3)
    ).astype(BF)
    rounded = direction.astype(BF)
    for d in range(blocks):
        send_ref[d, :, :chunk] = rounded
        send_ref[d, :, chunk:] = stats
    feature_ref[...] = feature
    root_ref[...] = jnp.broadcast_to(root, (FR, LANES))


def spread_kernel(
    blocks,
    chunk,
    width,
    tokens,
    got_ref,
    w_ref,
    pooled_ref,
    meta_ref,
    root_ref,
    feature_ref,
    picked_ref,
    spread_ref,
    heads_ref,
):
    meta = meta_ref[...]
    count = jnp.maximum(take_lanes(meta, 0, 1), 1.0)
    weight = take_lanes(meta, 1, 1)
    root = take_lanes(root_ref[...], 0, 1)
    stats = got_ref[0, :, chunk:].astype(F32)
    for d in range(1, blocks):
        stats = stats + got_ref[d, :, chunk:].astype(F32)
    score = take_lanes(stats, 0, 3)
    slope = take_lanes(stats, 3, 3)
    grad_score = -weight * jax.nn.sigmoid(-score) / FRAMES
    total = jnp.zeros(pooled_ref.shape, F32)
    for d in range(blocks):
        total = total + dot_nt(got_ref[d, :, :chunk], w_chunk(w_ref, d, chunk))
    grad_root = -(grad_score * slope) / root
    grad_pooled = (grad_score / root) * total + (grad_root / root / width) * pooled_ref[...]
    spread_ref[:FR] = (tokens * (grad_pooled / count)).astype(BF)
    spread_ref[FR:] = jnp.zeros((LANES - FR, pooled_ref.shape[1]), BF)
    scaled = feature_ref[...] * grad_score
    picked = picked_ref[...]
    for j in range(NDH):
        heads_ref[j : j + 1, :] = jnp.sum(scaled * picked[:, j : j + 1], axis=0, keepdims=True)


def output_kernel(q_ref, k_ref, v_ref, aug_ref, o_ref):
    blocks = q_ref.shape[0]
    tokens = blocks * LANES
    chunk = row_chunk(tokens)
    per = chunk // LANES
    keys = jnp.concatenate([rows_of(k_ref), ones_three((tokens, LANES))], axis=1)
    values = rows_of(v_ref)

    def step(i, carry):
        q = q_ref[pl.ds(i * per, per)].reshape(chunk, HS)
        aug = aug_ref[0, pl.ds(pl.multiple_of(i * chunk, chunk), chunk)]
        s = dot_nt(jnp.concatenate([q, aug], axis=1), keys)
        p = jnp.exp2(s * (SCALE * LOG2E)).astype(BF)
        o = dot_nn(p, values).astype(BF)
        o_ref[pl.ds(i * per, per)] = o.reshape(per, LANES, HS)
        return carry

    run_steps(tokens // chunk, step, 0)


def back_kernel(q_ref, k_ref, v_ref, o_ref, aug_ref, m_ref, spread_ref, dqk_ref, dk_ref):
    blocks = q_ref.shape[0]
    tokens = blocks * LANES
    chunk = row_chunk(tokens)
    per = chunk // LANES
    plain = rows_of(k_ref)
    keys = jnp.concatenate([plain, ones_three((tokens, LANES))], axis=1)
    values = rows_of(v_ref)
    spread = spread_ref[...]
    dk_ref[...] = jnp.zeros(dk_ref.shape, F32)

    def step(i, carry):
        at = pl.ds(pl.multiple_of(i * chunk, chunk), chunk)
        q = q_ref[pl.ds(i * per, per)].reshape(chunk, HS)
        o = o_ref[pl.ds(i * per, per)].reshape(chunk, HS)
        s = dot_nt(jnp.concatenate([q, aug_ref[0, at]], axis=1), keys)
        p = jnp.exp2(s * (SCALE * LOG2E))
        grad = dot_nn(m_ref[at], spread)
        delta = jnp.sum(grad * o.astype(F32), axis=1, keepdims=True)
        dp = dot_nt(grad.astype(BF), values)
        ds = (p * (dp - delta)).astype(BF)
        dq = (dot_nn(ds, plain) * SCALE).astype(BF)
        dqk_ref[pl.ds(i * per, per), :LANES] = dq.reshape(per, LANES, HS)
        dk_ref[...] += dot_tn(ds, q)
        return carry

    run_steps(tokens // chunk, step, 0)
    dk = (dk_ref[...] * SCALE).astype(BF)
    dqk_ref[:, LANES:] = dk.reshape(blocks, LANES, HS)


def value_kernel(heads, r_ref, spread_ref, dv_ref):
    for h in range(heads):
        at = slice(h * HS, (h + 1) * HS)
        dv_ref[:, at] = dot_tn(r_ref[0, h], spread_ref[0, :, at]).astype(BF)


def exchange(array):
    return lax.all_to_all(array, "gen", split_axis=0, concat_axis=0, tiled=True)


def on_device(
    query_in, key_in, value_in, teacher_w, disc_heads, frame_of_token, head_of_frame, timestep
):
    n = lax.axis_size("gen")
    grp = lax.axis_size("grp")
    me = lax.axis_index("gen")
    tok = query_in.shape[1]
    width = query_in.shape[2]
    tokens = tok * n
    heads = width // HS // n
    lw = heads * HS
    dh = teacher_w.shape[1]
    columns = dh // n
    chunk = -(-columns // LANES) * LANES
    rows = row_chunk(tokens)

    def to_blocks(array):
        return jnp.transpose(array.reshape(tok, n, lw), (1, 0, 2))

    qk = exchange(jnp.concatenate([to_blocks(query_in[0]), to_blocks(key_in[0])], axis=1))
    v = exchange(to_blocks(value_in[0]))

    frames = frame_of_token[0]
    member = (frames[:, None] == lax.broadcasted_iota(jnp.int32, (tokens, LANES), 1)).astype(BF)
    member_t = (
        frames[None, :] == lax.broadcasted_iota(jnp.int32, (FR, tokens), 0)
    )
    counts = jnp.sum(member_t.astype(F32), axis=1)
    member_t = jnp.transpose(
        member_t.astype(BF).reshape(FR, tokens // rows, rows), (1, 0, 2)
    )
    weight = (timestep[0].astype(F32) + 1.0) / NSTEPS
    lane = lax.broadcasted_iota(jnp.int32, (FR, LANES), 1)
    meta = jnp.where(lane == 0, counts[:, None], weight)
    head_ids = jnp.concatenate([head_of_frame[0], jnp.full((FR - FRAMES,), NDH, jnp.int32)])
    picked = (
        head_ids[:, None] == lax.broadcasted_iota(jnp.int32, (FR, NDH), 1)
    ).astype(F32)
    my_heads = lax.dynamic_slice_in_dim(disc_heads, me * columns, columns, axis=1)
    my_heads = jnp.pad(my_heads, ((0, 0), (0, chunk - columns)))
    head_rows = jnp.sum(picked[:, :, None] * my_heads[None], axis=1)
    if chunk == columns:
        w = teacher_w
    else:
        w = jnp.transpose(teacher_w.reshape(lw, n, columns), (1, 0, 2))
        w = jnp.pad(w, ((0, 0), (0, 0), (0, chunk - columns)))

    head_block = pl.BlockSpec((n, LANES, HS), lambda h: (0, 0, h))
    second_block = pl.BlockSpec((n, LANES, HS), lambda h: (0, 1, h))
    aug_block = pl.BlockSpec((1, tokens, LANES), lambda h: (h, 0, 0))
    square = 2 * tokens * tokens * HS

    with jax.named_scope("softmax_stats"):
        aug, r = pl.pallas_call(
            stats_kernel,
            grid=(heads,),
            in_specs=[
                head_block,
                second_block,
                pl.BlockSpec((tokens // rows, FR, rows), lambda h: (0, 0, 0)),
            ],
            out_specs=[
                aug_block,
                pl.BlockSpec((n, 1, FR, LANES), lambda h: (0, h, 0, 0)),
            ],
            out_shape=[
                jax.ShapeDtypeStruct((heads, tokens, LANES), BF),
                jax.ShapeDtypeStruct((n, heads, FR, LANES), BF),
            ],
            compiler_params=params(),
            cost_estimate=pl.CostEstimate(
                flops=heads * square, bytes_accessed=4 << 20, transcendentals=heads * tokens**2
            ),
        )(qk, qk, member_t)

    with jax.named_scope("pool_project"):
        part, pooled = pl.pallas_call(
            functools.partial(pool_kernel, n, heads, chunk),
            out_shape=[
                jax.ShapeDtypeStruct((n, FR, chunk + LANES), BF),
                jax.ShapeDtypeStruct((FR, lw), F32),
            ],
            compiler_params=params(0),
        )(r, v, meta, w)

    got = exchange(part)

    with jax.named_scope("attention_output"):
        mixed = pl.pallas_call(
            output_kernel,
            grid=(heads,),
            in_specs=[head_block, second_block, head_block, aug_block],
            out_specs=head_block,
            out_shape=jax.ShapeDtypeStruct((n, LANES, lw), BF),
            compiler_params=params(),
            cost_estimate=pl.CostEstimate(
                flops=2 * heads * square, bytes_accessed=5 << 20, transcendentals=heads * tokens**2
            ),
        )(qk, qk, v, aug)

    with jax.named_scope("discriminator"):
        send, feature, root = pl.pallas_call(
            functools.partial(middle_kernel, n, chunk, width),
            out_shape=[
                jax.ShapeDtypeStruct((n, FR, chunk + LANES), BF),
                jax.ShapeDtypeStruct((FR, chunk), F32),
                jax.ShapeDtypeStruct((FR, LANES), F32),
            ],
            compiler_params=params(0),
        )(got, head_rows)

    got_back = exchange(send)

    with jax.named_scope("pooled_gradient"):
        spread, head_part = pl.pallas_call(
            functools.partial(spread_kernel, n, chunk, width, tokens),
            out_shape=[
                jax.ShapeDtypeStruct((LANES, lw), BF),
                jax.ShapeDtypeStruct((NDH, chunk), F32),
            ],
            compiler_params=params(0),
        )(got_back, w, pooled, meta, root, feature, picked)

    latents = exchange(mixed)

    with jax.named_scope("attention_back"):
        dqk = pl.pallas_call(
            back_kernel,
            grid=(heads,),
            in_specs=[
                head_block,
                second_block,
                head_block,
                head_block,
                aug_block,
                pl.BlockSpec((tokens, LANES), lambda h: (0, 0)),
                pl.BlockSpec((LANES, HS), lambda h: (0, h)),
            ],
            out_specs=pl.BlockSpec((n, 2 * LANES, HS), lambda h: (0, 0, h)),
            out_shape=jax.ShapeDtypeStruct((n, 2 * LANES, lw), BF),
            scratch_shapes=[pltpu.VMEM((tokens, HS), F32)],
            compiler_params=params(),
            cost_estimate=pl.CostEstimate(
                flops=4 * heads * square, bytes_accessed=8 << 20, transcendentals=heads * tokens**2
            ),
        )(qk, qk, v, mixed, aug, member, spread)

    step = 1
    while step < grp:
        head_part = head_part + lax.ppermute(
            head_part, "grp", [(i, i ^ step) for i in range(grp)]
        )
        step *= 2
    high = head_part.astype(BF)
    low = (head_part - high.astype(F32)).astype(BF)
    pieces = jnp.concatenate(
        [
            r.reshape(n, heads * FR, LANES),
            jnp.broadcast_to(
                jnp.transpose(spread[:FR].reshape(FR, heads, HS), (1, 0, 2)).reshape(
                    1, heads * FR, HS
                ),
                (n, heads * FR, HS),
            ),
            jnp.broadcast_to(
                jnp.concatenate([high, low], axis=0).reshape(1, -1, LANES),
                (n, 2 * NDH * chunk // LANES, LANES),
            ),
        ],
        axis=1,
    )
    pieces = exchange(pieces)
    all_r = pieces[:, : heads * FR].reshape(n, heads, FR, LANES)
    all_spread = jnp.transpose(
        pieces[:, heads * FR : 2 * heads * FR].reshape(n, heads, FR, HS), (0, 2, 1, 3)
    ).reshape(n, FR, lw)
    gathered = pieces[:, 2 * heads * FR :].reshape(n, 2, NDH, chunk).astype(F32)
    gathered = (gathered[:, 0] + gathered[:, 1])[:, :, :columns]
    grad_heads = jnp.transpose(gathered, (1, 0, 2)).reshape(NDH, dh)

    with jax.named_scope("value_gradient"):
        out_value = pl.pallas_call(
            functools.partial(value_kernel, heads),
            grid=(n,),
            in_specs=[
                pl.BlockSpec((1, heads, FR, LANES), lambda d: (d, 0, 0, 0)),
                pl.BlockSpec((1, FR, lw), lambda d: (d, 0, 0)),
            ],
            out_specs=pl.BlockSpec((tok, lw), lambda d: (0, d)),
            out_shape=jax.ShapeDtypeStruct((tok, width), BF),
            compiler_params=params(),
        )(all_r, all_spread)

    back = exchange(dqk)

    def to_tokens(blocks):
        return jnp.transpose(blocks, (1, 0, 2)).reshape(1, tok, width)

    return (
        to_tokens(latents),
        to_tokens(back[:, :LANES]),
        to_tokens(back[:, LANES:]),
        out_value[None],
        grad_heads,
    )


def solution(mesh):
    return jax.shard_map(
        on_device,
        mesh=mesh,
        in_specs=(
            P("grp", "gen", None),
            P("grp", "gen", None),
            P("grp", "gen", None),
            P("gen", None),
            P(),
            P("grp", None),
            P("grp", None),
            P("grp"),
        ),
        out_specs=(
            P("grp", "gen", None),
            P("grp", "gen", None),
            P("grp", "gen", None),
            P("grp", "gen", None),
            P(),
        ),
        check_vma=False,
    )
```

```python
import functools
import math

import jax
import jax.numpy as jnp
from jax import lax
from jax.experimental import pallas as pl
from jax.experimental.pallas import tpu as pltpu
from jax.sharding import PartitionSpec as P

HS = 128
FRAMES = 21
FR = 24
RR = 32
NDH = 8
NSTEPS = 1000
LANES = 128
epsilon = 1e-06
SCALE = 1.0 / math.sqrt(HS)
LOG2E = math.log2(math.e)
BF = jnp.bfloat16
F32 = jnp.float32


def params(tokens, axes=1):
    return pltpu.CompilerParams(
        vmem_limit_bytes=min(48, 16 * -(-tokens // 1024)) * 1024 * 1024,
        dimension_semantics=("arbitrary",) * axes,
    )


def hbm(array):
    return pltpu.with_memory_space_constraint(array, pltpu.HBM)


def after(value, *earlier):
    return lax.optimization_barrier((value,) + earlier)[0]


def dot_nn(a, b):
    return lax.dot_general(a, b, (((1,), (0,)), ((), ())), preferred_element_type=F32)


def dot_nt(a, b):
    return lax.dot_general(a, b, (((1,), (1,)), ((), ())), preferred_element_type=F32)


def dot_tn(a, b):
    return lax.dot_general(a, b, (((0,), (0,)), ((), ())), preferred_element_type=F32)


def rows_of(ref):
    block = ref[...]
    return block.reshape(block.shape[-3] * block.shape[-2], block.shape[-1])


def split_three(value):
    high = value.astype(BF)
    rest = value - high.astype(F32)
    middle = rest.astype(BF)
    low = (rest - middle.astype(F32)).astype(BF)
    return high, middle, low


def lanes_three(value, shape, first):
    lane = lax.broadcasted_iota(jnp.int32, shape, 1)
    out = jnp.zeros(shape, F32)
    for i, part in enumerate(split_three(value)):
        out = jnp.where(lane == first + i, part.astype(F32), out)
    return out


def ones_three(shape):
    lane = lax.broadcasted_iota(jnp.int32, shape, 1)
    return jnp.where(lane < 3, 1.0, 0.0).astype(BF)


def take_lanes(block, first, count):
    lane = lax.broadcasted_iota(jnp.int32, block.shape, 1)
    keep = (lane >= first) & (lane < first + count)
    return jnp.sum(jnp.where(keep, block, 0.0), axis=1, keepdims=True)


def row_chunk(tokens):
    return min(256, tokens)


def run_steps(count, step, carry):
    if count <= 4:
        for i in range(count):
            carry = step(i, carry)
        return carry
    return lax.fori_loop(0, count, step, carry)


def chunk_rows(i, chunk):
    return pl.ds(pl.multiple_of(i * chunk, chunk), chunk)


def stats_kernel(blocks, *refs):
    qk_refs, (mt_ref, aug_ref, r_ref, q_ref, k_ref) = refs[:blocks], refs[blocks:]
    tokens = blocks * LANES
    chunk = row_chunk(tokens)
    for s in range(blocks):
        at = slice(s * LANES, (s + 1) * LANES)
        q_ref[0, at] = qk_refs[s][0]
        k_ref[0, at] = qk_refs[s][1]
    keys = k_ref[0]

    def step(i, total_r):
        at = chunk_rows(i, chunk)
        s = dot_nt(q_ref[0, at], keys) * (SCALE * LOG2E)
        peak = jnp.max(s, axis=1, keepdims=True)
        e = jnp.exp2(s - peak)
        total = jnp.sum(e, axis=1, keepdims=True)
        p = (e * (1.0 / total)).astype(BF)
        lse = (peak + jnp.log2(total)) * (-1.0 / (SCALE * LOG2E))
        aug_ref[0, at] = lanes_three(lse, (chunk, LANES), 0).astype(BF)
        return total_r + dot_nn(mt_ref[i], p)

    r = run_steps(tokens // chunk, step, jnp.zeros((RR, tokens), F32))
    for s in range(blocks):
        r_ref[s, 0] = r[:, s * LANES : (s + 1) * LANES].astype(BF)


def pool_kernel(blocks, heads, chunk, *refs):
    v_refs, (r_ref, meta_ref, w_hbm, part_ref, pooled_ref, w_ref, sems) = (
        refs[:blocks],
        refs[blocks:],
    )
    copies = start_weights(w_hbm, w_ref, sems, blocks, chunk)
    count = jnp.maximum(take_lanes(meta_ref[...], 0, 1), 1.0)
    columns = []
    for h in range(heads):
        r = jnp.concatenate([r_ref[s, h] for s in range(blocks)], axis=1)
        v = jnp.concatenate(
            [v_refs[s][:, h * HS : (h + 1) * HS] for s in range(blocks)], axis=0
        )
        columns.append(dot_nn(r, v)[:FR])
    pooled = jnp.concatenate(columns, axis=1) if heads > 1 else columns[0]
    pooled = pooled / count
    pooled_ref[...] = pooled
    squares = jnp.sum(pooled * pooled, axis=1, keepdims=True)
    stats = lanes_three(squares, (FR, LANES), 0).astype(BF)
    rounded = pooled.astype(BF)
    for d in range(blocks):
        copies[d].wait()
        part_ref[d, :, :chunk] = dot_nn(rounded, w_ref[d]).astype(BF)
        part_ref[d, :, chunk:] = stats


def start_weights(w_hbm, w_ref, sems, blocks, chunk):
    copies = []
    for d in range(blocks):
        if len(w_hbm.shape) == 3:
            source = w_hbm.at[d]
        else:
            source = w_hbm.at[:, d * chunk : (d + 1) * chunk]
        copies.append(pltpu.make_async_copy(source, w_ref.at[d], sems.at[d]))
        copies[d].start()
    return copies


def middle_kernel(blocks, chunk, width, got_ref, rows_ref, send_ref, feature_ref, root_ref):
    total = got_ref[0].astype(F32)
    for d in range(1, blocks):
        total = total + got_ref[d].astype(F32)
    projected = total[:, :chunk]
    squares = take_lanes(total[:, chunk:], 0, 3)
    root = jnp.sqrt(squares / width + epsilon)
    pre = projected / root
    gate = jax.nn.sigmoid(pre)
    feature = pre * gate
    head_rows = rows_ref[...]
    direction = head_rows * gate * (1.0 + pre * (1.0 - gate))
    score = jnp.sum(feature * head_rows, axis=1, keepdims=True)
    slope = jnp.sum(direction * pre, axis=1, keepdims=True)
    stats = (
        lanes_three(score, (FR, LANES), 0) + lanes_three(slope, (FR, LANES), 3)
    ).astype(BF)
    rounded = direction.astype(BF)
    for d in range(blocks):
        send_ref[d, :, :chunk] = rounded
        send_ref[d, :, chunk:] = stats
    feature_ref[...] = feature
    root_ref[...] = jnp.broadcast_to(root, (FR, LANES))


def spread_kernel(
    blocks,
    chunk,
    width,
    tokens,
    got_ref,
    w_hbm,
    pooled_ref,
    meta_ref,
    root_ref,
    feature_ref,
    picked_ref,
    spread_ref,
    heads_ref,
    w_ref,
    sems,
):
    copies = start_weights(w_hbm, w_ref, sems, blocks, chunk)
    meta = meta_ref[...]
    count = jnp.maximum(take_lanes(meta, 0, 1), 1.0)
    weight = take_lanes(meta, 1, 1)
    root = take_lanes(root_ref[...], 0, 1)
    stats = got_ref[0, :, chunk:].astype(F32)
    for d in range(1, blocks):
        stats = stats + got_ref[d, :, chunk:].astype(F32)
    score = take_lanes(stats, 0, 3)
    slope = take_lanes(stats, 3, 3)
    grad_score = -weight * jax.nn.sigmoid(-score) / FRAMES
    total = jnp.zeros(pooled_ref.shape, F32)
    for d in range(blocks):
        copies[d].wait()
        total = total + dot_nt(got_ref[d, :, :chunk], w_ref[d])
    grad_root = -(grad_score * slope) / root
    grad_pooled = (grad_score / root) * total + (grad_root / root / width) * pooled_ref[...]
    spread_ref[:FR] = (tokens * (grad_pooled / count)).astype(BF)
    spread_ref[FR:] = jnp.zeros((LANES - FR, pooled_ref.shape[1]), BF)
    scaled = feature_ref[...] * grad_score
    picked = picked_ref[...]
    for j in range(NDH):
        heads_ref[j : j + 1, :] = jnp.sum(scaled * picked[:, j : j + 1], axis=0, keepdims=True)


def output_kernel(blocks, *refs):
    v_refs, (q_ref, k_ref, aug_ref, r_ref) = refs[:blocks], refs[blocks : blocks + 4]
    send_refs, (v_ref, o_ref) = refs[blocks + 4 : -2], refs[-2:]
    tokens = blocks * LANES
    chunk = row_chunk(tokens)
    for s in range(blocks):
        v_ref[0, s * LANES : (s + 1) * LANES] = v_refs[s][...]
    keys = jnp.concatenate([k_ref[0], ones_three((tokens, LANES))], axis=1)
    values = v_ref[0]

    def step(i, carry):
        at = chunk_rows(i, chunk)
        s = dot_nt(jnp.concatenate([q_ref[0, at], aug_ref[0, at]], axis=1), keys)
        p = jnp.exp2(s * (SCALE * LOG2E)).astype(BF)
        o_ref[0, at] = dot_nn(p, values).astype(BF)
        return carry

    run_steps(tokens // chunk, step, 0)
    for s in range(blocks):
        send_refs[s][:LANES] = o_ref[0, s * LANES : (s + 1) * LANES]
        send_refs[s][LANES:] = r_ref[s, 0]


def back_kernel(
    blocks, apart, q_ref, k_ref, v_ref, o_ref, aug_ref, m_ref, spread_ref, extra_ref, *refs
):
    out_refs, dk_ref, dq_ref = refs[:-2], refs[-2], refs[-1]
    tokens = blocks * LANES
    chunk = row_chunk(tokens)
    plain = k_ref[0]
    keys = jnp.concatenate([plain, ones_three((tokens, LANES))], axis=1)
    values = v_ref[0]
    spread = spread_ref[...]
    dk_ref[...] = jnp.zeros(dk_ref.shape, F32)

    def step(i, carry):
        at = chunk_rows(i, chunk)
        q = q_ref[0, at]
        s = dot_nt(jnp.concatenate([q, aug_ref[0, at]], axis=1), keys)
        p = jnp.exp2(s * (SCALE * LOG2E))
        grad = dot_nn(m_ref[at], spread)
        delta = jnp.sum(grad * o_ref[0, at].astype(F32), axis=1, keepdims=True)
        dp = dot_nt(grad.astype(BF), values)
        ds = (p * (dp - delta)).astype(BF)
        dq_ref[at] = (dot_nn(ds, plain) * SCALE).astype(BF)
        dk_ref[...] += dot_tn(ds, q)
        return carry

    run_steps(tokens // chunk, step, 0)
    dk = (dk_ref[...] * SCALE).astype(BF)
    me = lax.axis_index("gen")
    for s in range(blocks):
        at = slice(s * LANES, (s + 1) * LANES)
        out_ref = out_refs[s] if apart else out_refs[0].at[me ^ s]
        out_ref[:LANES] = dq_ref[at]
        out_ref[LANES : 2 * LANES] = dk[at]
        out_ref[2 * LANES : 2 * LANES + RR] = spread[:RR]
        if apart:
            out_ref[2 * LANES + RR :] = extra_ref[...]


def received(blocks, near_refs, far_refs, s):
    near = len(near_refs)
    if s < near:
        return [near_refs[s]]
    return [far_refs[i + s - near] for i in range(0, len(far_refs), blocks - near)]


def latent_kernel(blocks, lw, *refs):
    near = blocks - blocks // 2
    me = lax.axis_index("gen")
    for s in range(blocks):
        first = 0
        for ref in received(blocks, refs[:near], refs[near:-1], s):
            at = pl.ds(pl.multiple_of((me ^ s) * lw + first, LANES), ref.shape[1])
            refs[-1][:, at] = ref[:LANES]
            first += ref.shape[1]


def finish_kernel(blocks, lw, chunk, near, far, split, *refs):
    near_refs, far_refs = refs[:near], refs[near : near + far]
    late_refs, early_refs = refs[near + far :][:blocks], refs[near + far + blocks : -4]
    dq_ref, dk_ref, dv_ref, heads_ref = refs[-4:]
    me = lax.axis_index("gen")
    first = split * HS
    last = lw - first
    for s in range(blocks):
        d = me ^ s
        late = late_refs[s]
        at = pl.ds(pl.multiple_of(d * lw + first, LANES), last)
        dq_ref[:, at] = late[:LANES]
        dk_ref[:, at] = late[LANES : 2 * LANES]
        spreads = [late[2 * LANES : 2 * LANES + RR]]
        if split:
            at = pl.ds(pl.multiple_of(d * lw, LANES), first)
            early = early_refs[0].at[d]
            dq_ref[:, at] = early[:LANES]
            dk_ref[:, at] = early[LANES : 2 * LANES]
            spreads = [early[2 * LANES : 2 * LANES + RR]] + spreads
        rows = [ref[LANES:] for ref in received(blocks, near_refs, far_refs, s)]
        rows = jnp.concatenate(rows, axis=1) if len(rows) > 1 else rows[0]
        spread = jnp.concatenate(spreads, axis=1) if split else spreads[0]
        parts = [
            dot_tn(rows[:, h : h + HS], spread[:, h : h + HS]).astype(BF)
            for h in range(0, lw, HS)
        ]
        at = pl.ds(pl.multiple_of(d * lw, LANES), lw)
        dv_ref[:, at] = jnp.concatenate(parts, axis=1) if len(parts) > 1 else parts[0]
        per = last // LANES
        for piece in range(chunk // LANES):
            row = 2 * LANES + RR + piece // per * 2 * NDH
            lane = piece % per * LANES
            both = late[row : row + 2 * NDH, lane : lane + LANES].astype(F32)
            at = pl.ds(pl.multiple_of(d * chunk + piece * LANES, LANES), LANES)
            heads_ref[:, at] = both[:NDH] + both[NDH:]


def exchange(array):
    return lax.all_to_all(array, "gen", split_axis=0, concat_axis=0, tiled=True)


def on_device(
    query_in, key_in, value_in, teacher_w, disc_heads, frame_of_token, head_of_frame, timestep
):
    n = lax.axis_size("gen")
    grp = lax.axis_size("grp")
    me = lax.axis_index("gen")
    tok = query_in.shape[1]
    width = query_in.shape[2]
    tokens = tok * n
    heads = width // HS // n
    lw = heads * HS
    dh = teacher_w.shape[1]
    columns = dh // n
    chunk = -(-columns // LANES) * LANES
    rows = row_chunk(tokens)

    far, near = list(range(n // 2, n)), list(range(1, n // 2))
    half = len(far)

    def columns_for(array, s):
        return lax.dynamic_slice_in_dim(array, (me ^ s) * lw, lw, axis=1)

    def send(array, s):
        return lax.ppermute(array, "gen", [(i, i ^ s) for i in range(n)])

    def query_key(s):
        return jnp.stack([columns_for(query_in[0], s), columns_for(key_in[0], s)])

    qk, v = {0: query_key(0)}, {0: columns_for(value_in[0], 0)}
    blocks = {s: query_key(s) for s in far}
    for s in far:
        qk[s] = send(blocks[s], s)
    most = [qk[s] for s in far[: half - 1]]
    every = [qk[s] for s in far]
    for s in near:
        behind = [qk[s - 1]] if s > 1 else list(blocks.values())
        qk[s] = send(after(query_key(s), *behind), s)
    for s in near:
        behind = v[s - 1] if s > 1 else qk[s]
        v[s] = send(after(columns_for(value_in[0], s), behind), s)
    for i, s in enumerate(far):
        v[s] = send(after(columns_for(value_in[0], s), *(most if i < 2 else every)), s)
    qk, v = [qk[s] for s in range(n)], [v[s] for s in range(n)]

    frames = frame_of_token[0]
    frames = jnp.take(frames.reshape(n, tok), me ^ jnp.arange(n), axis=0).reshape(tokens)
    member = (frames[:, None] == lax.broadcasted_iota(jnp.int32, (tokens, LANES), 1)).astype(BF)
    member_t = (
        frames[None, :] == lax.broadcasted_iota(jnp.int32, (RR, tokens), 0)
    )
    counts = jnp.sum(member_t.astype(F32), axis=1)[:FR]
    member_t = jnp.transpose(
        member_t.astype(BF).reshape(RR, tokens // rows, rows), (1, 0, 2)
    )
    weight = (timestep[0].astype(F32) + 1.0) / NSTEPS
    lane = lax.broadcasted_iota(jnp.int32, (FR, LANES), 1)
    meta = jnp.where(lane == 0, counts[:, None], weight)
    head_ids = jnp.concatenate([head_of_frame[0], jnp.full((FR - FRAMES,), NDH, jnp.int32)])
    picked = (
        head_ids[:, None] == lax.broadcasted_iota(jnp.int32, (FR, NDH), 1)
    ).astype(F32)
    my_heads = lax.dynamic_slice_in_dim(disc_heads, me * columns, columns, axis=1)
    my_heads = jnp.pad(my_heads, ((0, 0), (0, chunk - columns)))
    head_rows = jnp.sum(picked[:, :, None] * my_heads[None], axis=1)
    if chunk == columns:
        w = teacher_w
    else:
        w = jnp.transpose(teacher_w.reshape(lw, n, columns), (1, 0, 2))
        w = jnp.pad(w, ((0, 0), (0, 0), (0, chunk - columns)))

    head_block = pl.BlockSpec((1, tokens, HS), lambda h: (h, 0, 0))
    head_shape = pltpu.HBM((heads, tokens, HS), BF)
    r_block = pl.BlockSpec((n, 1, RR, LANES), lambda h: (0, h, 0, 0))
    square = 2 * tokens * tokens * HS
    in_vmem = pl.BlockSpec(memory_space=pltpu.VMEM)
    anywhere = pl.BlockSpec(memory_space=pl.ANY)
    weights_scratch = [pltpu.VMEM((n, lw, chunk), BF), pltpu.SemaphoreType.DMA((n,))]

    with jax.named_scope("softmax_stats"):
        aug, r, q_rows, k_rows = pl.pallas_call(
            functools.partial(stats_kernel, n),
            grid=(heads,),
            in_specs=[pl.BlockSpec((2, LANES, HS), lambda h: (0, 0, h))] * n
            + [pl.BlockSpec((tokens // rows, RR, rows), lambda h: (0, 0, 0))],
            out_specs=[head_block, r_block, head_block, head_block],
            out_shape=[
                head_shape,
                pltpu.HBM((n, heads, RR, LANES), BF),
                head_shape,
                head_shape,
            ],
            compiler_params=params(tokens),
            cost_estimate=pl.CostEstimate(
                flops=heads * square, bytes_accessed=4 << 20, transcendentals=heads * tokens**2
            ),
        )(*map(hbm, qk), member_t)

    with jax.named_scope("pool_project"):
        part, pooled = pl.pallas_call(
            functools.partial(pool_kernel, n, heads, chunk),
            in_specs=[in_vmem] * (n + 2) + [anywhere],
            scratch_shapes=weights_scratch,
            out_shape=[
                jax.ShapeDtypeStruct((n, FR, chunk + LANES), BF),
                jax.ShapeDtypeStruct((FR, lw), F32),
            ],
            compiler_params=params(tokens, 0),
        )(*v, r, meta, hbm(w))

    got = exchange(part)

    split = heads // 2
    parts = [(0, split), (split, heads)] if split else [(0, heads)]

    def output(first, last, behind):
        at = pl.BlockSpec((1, tokens, HS), lambda h: (h + first, 0, 0))
        own = pltpu.HBM((last - first, tokens, HS), BF)
        with jax.named_scope("attention_output"):
            *made, v_rows, o_rows = pl.pallas_call(
                functools.partial(output_kernel, n),
                grid=(last - first,),
                in_specs=[pl.BlockSpec((LANES, HS), lambda h: (0, h + first))] * n
                + [at] * 3
                + [pl.BlockSpec((n, 1, RR, LANES), lambda h: (0, h + first, 0, 0))],
                out_specs=[pl.BlockSpec((LANES + RR, HS), lambda h: (0, h))] * n
                + [head_block, head_block],
                out_shape=[pltpu.HBM((LANES + RR, (last - first) * HS), BF)] * n + [own, own],
                compiler_params=params(tokens),
                cost_estimate=pl.CostEstimate(
                    flops=2 * (last - first) * square,
                    bytes_accessed=(last - first) << 20,
                    transcendentals=(last - first) * tokens**2,
                ),
            )(*map(hbm, v), *map(hbm, (q_rows, k_rows, aug, after(r, behind))))
        return made, v_rows, o_rows

    outputs = [output(*parts[0], part)]
    got = after(got, outputs[0][2])
    mixed = [[send(outputs[0][0][s], s) for s in far]]

    with jax.named_scope("discriminator"):
        direction, feature, root = pl.pallas_call(
            functools.partial(middle_kernel, n, chunk, width),
            out_shape=[
                jax.ShapeDtypeStruct((n, FR, chunk + LANES), BF),
                jax.ShapeDtypeStruct((FR, chunk), F32),
                jax.ShapeDtypeStruct((FR, LANES), F32),
            ],
            compiler_params=params(tokens, 0),
        )(got, head_rows)

    got_back = exchange(after(direction, *mixed[0][:2]))
    got_back = after(got_back, *mixed[0][2:])
    if split:
        outputs.append(output(*parts[1], direction))
        got_back = after(got_back, outputs[1][2])
        mixed.append([send(outputs[1][0][s], s) for s in far])
    mixed_near = []
    for s in range(n - half):
        block = jnp.concatenate([made[0][s] for made in outputs], axis=1) if split else outputs[0][0][s]
        mixed_near.append(send(block, s) if s else block)

    with jax.named_scope("pooled_gradient"):
        spread, head_part = pl.pallas_call(
            functools.partial(spread_kernel, n, chunk, width, tokens),
            in_specs=[in_vmem, anywhere] + [in_vmem] * 5,
            scratch_shapes=weights_scratch,
            out_shape=[
                jax.ShapeDtypeStruct((LANES, lw), BF),
                jax.ShapeDtypeStruct((NDH, chunk), F32),
            ],
            compiler_params=params(tokens, 0),
        )(got_back, hbm(w), pooled, meta, root, feature, picked)

    def back(i, apart, extra):
        first, last = parts[i]
        part = (last - first) * HS
        if apart:
            block = (2 * LANES + RR + extra.shape[0], HS)
        else:
            block = (n, 2 * LANES + RR, HS)
        shape = block[:-1] + (part,)
        count = n if apart else 1
        at = pl.BlockSpec((1, tokens, HS), lambda h: (h + first, 0, 0))
        with jax.named_scope("attention_back"):
            return pl.pallas_call(
                functools.partial(back_kernel, n, apart),
                grid=(last - first,),
                in_specs=[at, at, head_block, head_block, at]
                + [
                    pl.BlockSpec((tokens, LANES), lambda h: (0, 0)),
                    pl.BlockSpec((LANES, HS), lambda h: (0, h + first)),
                    pl.BlockSpec((extra.shape[0], HS), lambda h: (0, h)),
                ],
                out_specs=[pl.BlockSpec(block, lambda h: (0,) * (len(block) - 1) + (h,))] * count,
                out_shape=[pltpu.HBM(shape, BF)] * count,
                scratch_shapes=[pltpu.VMEM((tokens, HS), F32), pltpu.VMEM((tokens, HS), BF)],
                compiler_params=params(tokens),
                cost_estimate=pl.CostEstimate(
                    flops=4 * (last - first) * square,
                    bytes_accessed=(last - first) * (2 << 20),
                    transcendentals=(last - first) * tokens**2,
                ),
            )(*map(hbm, (q_rows, k_rows) + outputs[i][1:] + (aug,)), member, spread, extra)

    early = []
    if split:
        made = back(0, False, jnp.zeros((2 * NDH, split * HS), BF))[0]
        spread, head_part, made = lax.optimization_barrier((spread, head_part, made))
        made = after(made, *(block for blocks in mixed for block in blocks), *mixed_near[1:])
        early = [exchange(made)]

    step = 1
    while step < grp:
        head_part = head_part + lax.ppermute(
            head_part, "grp", [(i, i ^ step) for i in range(grp)]
        )
        step *= 2
    high = head_part.astype(BF)
    low = (head_part - high.astype(F32)).astype(BF)
    late_width = lw - split * HS
    groups = -(-chunk // late_width)
    extra = jnp.concatenate([high, low], axis=0)
    extra = jnp.pad(extra, ((0, 0), (0, groups * late_width - chunk)))
    extra = jnp.transpose(extra.reshape(2 * NDH, groups, late_width), (1, 0, 2))
    made = back(len(parts) - 1, True, extra.reshape(groups * 2 * NDH, late_width))
    late = [made[0]] + [send(made[s], s) for s in range(1, n)]

    whole = jax.ShapeDtypeStruct((tok, width), BF)
    mixed = mixed_near + [block for blocks in mixed for block in blocks]
    with jax.named_scope("latents"):
        latents = pl.pallas_call(
            functools.partial(latent_kernel, n, lw),
            out_shape=whole,
            compiler_params=params(tokens, 0),
        )(*map(hbm, mixed))
    with jax.named_scope("finish"):
        late[0] = after(late[0], latents)
        out_query, out_key, out_value, grad_heads = pl.pallas_call(
            functools.partial(
                finish_kernel, n, lw, chunk, n - half, len(mixed) - (n - half), split
            ),
            out_shape=[whole] * 3 + [jax.ShapeDtypeStruct((NDH, n * chunk), F32)],
            compiler_params=params(tokens, 0),
        )(*map(hbm, mixed + late + early))
    if chunk != columns:
        grad_heads = grad_heads.reshape(NDH, n, chunk)[:, :, :columns].reshape(NDH, dh)

    return (latents[None], out_query[None], out_key[None], out_value[None], grad_heads)


def solution(mesh):
    return jax.shard_map(
        on_device,
        mesh=mesh,
        in_specs=(
            P("grp", "gen", None),
            P("grp", "gen", None),
            P("grp", "gen", None),
            P("gen", None),
            P(),
            P("grp", None),
            P("grp", None),
            P("grp"),
        ),
        out_specs=(
            P("grp", "gen", None),
            P("grp", "gen", None),
            P("grp", "gen", None),
            P("grp", "gen", None),
            P(),
        ),
        check_vma=False,
    )
```

```python
import functools
import math

import jax
import jax.numpy as jnp
from jax import lax
from jax.experimental import pallas as pl
from jax.experimental.pallas import tpu as pltpu
from jax.sharding import PartitionSpec as P

HS = 128
FRAMES = 21
FR = 24
RR = 32
NDH = 8
NSTEPS = 1000
LANES = 128
epsilon = 1e-06
SCALE = 1.0 / math.sqrt(HS)
LOG2E = math.log2(math.e)
BF = jnp.bfloat16
F32 = jnp.float32


def params(tokens, axes=1):
    return pltpu.CompilerParams(
        vmem_limit_bytes=min(48, 16 * -(-tokens // 1024)) * 1024 * 1024,
        dimension_semantics=("arbitrary",) * axes,
    )


def hbm(array):
    return pltpu.with_memory_space_constraint(array, pltpu.HBM)


def after(value, *earlier):
    return lax.optimization_barrier((value,) + earlier)[0]


def dot_nn(a, b):
    return lax.dot_general(a, b, (((1,), (0,)), ((), ())), preferred_element_type=F32)


def dot_nt(a, b):
    return lax.dot_general(a, b, (((1,), (1,)), ((), ())), preferred_element_type=F32)


def dot_tn(a, b):
    return lax.dot_general(a, b, (((0,), (0,)), ((), ())), preferred_element_type=F32)


def rows_of(ref):
    block = ref[...]
    return block.reshape(block.shape[-3] * block.shape[-2], block.shape[-1])


def split_three(value):
    high = value.astype(BF)
    rest = value - high.astype(F32)
    middle = rest.astype(BF)
    low = (rest - middle.astype(F32)).astype(BF)
    return high, middle, low


def lanes_three(value, shape, first):
    lane = lax.broadcasted_iota(jnp.int32, shape, 1)
    out = jnp.zeros(shape, F32)
    for i, part in enumerate(split_three(value)):
        out = jnp.where(lane == first + i, part.astype(F32), out)
    return out


def ones_three(shape):
    lane = lax.broadcasted_iota(jnp.int32, shape, 1)
    return jnp.where(lane < 3, 1.0, 0.0).astype(BF)


def take_lanes(block, first, count):
    lane = lax.broadcasted_iota(jnp.int32, block.shape, 1)
    keep = (lane >= first) & (lane < first + count)
    return jnp.sum(jnp.where(keep, block, 0.0), axis=1, keepdims=True)


def row_chunk(tokens):
    return min(256, tokens)


def run_steps(count, step, carry):
    if count <= 4:
        for i in range(count):
            carry = step(i, carry)
        return carry
    return lax.fori_loop(0, count, step, carry)


def chunk_rows(i, chunk):
    return pl.ds(pl.multiple_of(i * chunk, chunk), chunk)


def stats_kernel(blocks, *refs):
    qk_refs, (mt_ref, aug_ref, r_ref, q_ref, k_ref) = refs[:blocks], refs[blocks:]
    tokens = blocks * LANES
    chunk = row_chunk(tokens)
    for s in range(blocks):
        at = slice(s * LANES, (s + 1) * LANES)
        q_ref[0, at] = qk_refs[s][0]
        k_ref[0, at] = qk_refs[s][1]
    keys = k_ref[0]

    def step(i, total_r):
        at = chunk_rows(i, chunk)
        s = dot_nt(q_ref[0, at], keys) * (SCALE * LOG2E)
        peak = jnp.max(s, axis=1, keepdims=True)
        e = jnp.exp2(s - peak)
        total = jnp.sum(e, axis=1, keepdims=True)
        p = (e * (1.0 / total)).astype(BF)
        lse = (peak + jnp.log2(total)) * (-1.0 / (SCALE * LOG2E))
        aug_ref[0, at] = lanes_three(lse, (chunk, LANES), 0).astype(BF)
        return total_r + dot_nn(mt_ref[i], p)

    r = run_steps(tokens // chunk, step, jnp.zeros((RR, tokens), F32))
    for s in range(blocks):
        r_ref[s, 0] = r[:FR, s * LANES : (s + 1) * LANES].astype(BF)


def pool_kernel(blocks, heads, chunk, *refs):
    v_refs, (r_ref, meta_ref, w_hbm, part_ref, pooled_ref, w_ref, sems) = (
        refs[:blocks],
        refs[blocks:],
    )
    copies = start_weights(w_hbm, w_ref, sems, blocks, chunk)
    count = jnp.maximum(take_lanes(meta_ref[...], 0, 1), 1.0)
    columns = []
    for h in range(heads):
        r = jnp.concatenate([r_ref[s, h] for s in range(blocks)], axis=1)
        v = jnp.concatenate(
            [v_refs[s][:, h * HS : (h + 1) * HS] for s in range(blocks)], axis=0
        )
        columns.append(dot_nn(r, v))
    pooled = jnp.concatenate(columns, axis=1) if heads > 1 else columns[0]
    pooled = pooled / count
    pooled_ref[...] = pooled
    squares = jnp.sum(pooled * pooled, axis=1, keepdims=True)
    stats = lanes_three(squares, (FR, LANES), 0).astype(BF)
    rounded = pooled.astype(BF)
    for d in range(blocks):
        copies[d].wait()
        part_ref[d, :, :chunk] = dot_nn(rounded, w_ref[d]).astype(BF)
        part_ref[d, :, chunk:] = stats


def start_weights(w_hbm, w_ref, sems, blocks, chunk):
    copies = []
    for d in range(blocks):
        if len(w_hbm.shape) == 3:
            source = w_hbm.at[d]
        else:
            source = w_hbm.at[:, d * chunk : (d + 1) * chunk]
        copies.append(pltpu.make_async_copy(source, w_ref.at[d], sems.at[d]))
        copies[d].start()
    return copies


def middle_kernel(blocks, chunk, width, got_ref, rows_ref, send_ref, feature_ref, root_ref):
    total = got_ref[0].astype(F32)
    for d in range(1, blocks):
        total = total + got_ref[d].astype(F32)
    projected = total[:, :chunk]
    squares = take_lanes(total[:, chunk:], 0, 3)
    root = jnp.sqrt(squares / width + epsilon)
    pre = projected / root
    gate = jax.nn.sigmoid(pre)
    feature = pre * gate
    head_rows = rows_ref[...]
    direction = head_rows * gate * (1.0 + pre * (1.0 - gate))
    score = jnp.sum(feature * head_rows, axis=1, keepdims=True)
    slope = jnp.sum(direction * pre, axis=1, keepdims=True)
    stats = (
        lanes_three(score, (FR, LANES), 0) + lanes_three(slope, (FR, LANES), 3)
    ).astype(BF)
    rounded = direction.astype(BF)
    for d in range(blocks):
        send_ref[d, :, :chunk] = rounded
        send_ref[d, :, chunk:] = stats
    feature_ref[...] = feature
    root_ref[...] = jnp.broadcast_to(root, (FR, LANES))


def spread_kernel(
    blocks,
    chunk,
    width,
    tokens,
    got_ref,
    w_hbm,
    pooled_ref,
    meta_ref,
    root_ref,
    feature_ref,
    picked_ref,
    spread_ref,
    heads_ref,
    w_ref,
    sems,
):
    copies = start_weights(w_hbm, w_ref, sems, blocks, chunk)
    meta = meta_ref[...]
    count = jnp.maximum(take_lanes(meta, 0, 1), 1.0)
    weight = take_lanes(meta, 1, 1)
    root = take_lanes(root_ref[...], 0, 1)
    stats = got_ref[0, :, chunk:].astype(F32)
    for d in range(1, blocks):
        stats = stats + got_ref[d, :, chunk:].astype(F32)
    score = take_lanes(stats, 0, 3)
    slope = take_lanes(stats, 3, 3)
    grad_score = -weight * jax.nn.sigmoid(-score) / FRAMES
    total = jnp.zeros(pooled_ref.shape, F32)
    for d in range(blocks):
        copies[d].wait()
        total = total + dot_nt(got_ref[d, :, :chunk], w_ref[d])
    grad_root = -(grad_score * slope) / root
    grad_pooled = (grad_score / root) * total + (grad_root / root / width) * pooled_ref[...]
    spread_ref[:FR] = (tokens * (grad_pooled / count)).astype(BF)
    spread_ref[FR:] = jnp.zeros((LANES - FR, pooled_ref.shape[1]), BF)
    scaled = feature_ref[...] * grad_score
    picked = picked_ref[...]
    for j in range(NDH):
        heads_ref[j : j + 1, :] = jnp.sum(scaled * picked[:, j : j + 1], axis=0, keepdims=True)


def output_kernel(blocks, *refs):
    v_refs, (q_ref, k_ref, aug_ref, r_ref) = refs[:blocks], refs[blocks : blocks + 4]
    send_refs, (v_ref, o_ref) = refs[-2 - blocks : -2], refs[-2:]
    tokens = blocks * LANES
    chunk = row_chunk(tokens)
    for s in range(blocks):
        v_ref[0, s * LANES : (s + 1) * LANES] = v_refs[s][...]
    keys = jnp.concatenate([k_ref[0], ones_three((tokens, LANES))], axis=1)
    values = v_ref[0]

    def step(i, carry):
        at = chunk_rows(i, chunk)
        s = dot_nt(jnp.concatenate([q_ref[0, at], aug_ref[0, at]], axis=1), keys)
        p = jnp.exp2(s * (SCALE * LOG2E)).astype(BF)
        o_ref[0, at] = dot_nn(p, values).astype(BF)
        return carry

    run_steps(tokens // chunk, step, 0)
    for s in range(blocks):
        send_refs[s][:LANES] = o_ref[0, s * LANES : (s + 1) * LANES]
        send_refs[s][LANES:] = r_ref[s, 0]


def back_kernel(
    blocks, apart, q_ref, k_ref, v_ref, o_ref, aug_ref, m_ref, spread_ref, extra_ref, *refs
):
    out_refs, dk_ref, dq_ref = refs[:-2], refs[-2], refs[-1]
    tokens = blocks * LANES
    chunk = row_chunk(tokens)
    count = tokens // chunk
    plain = k_ref[0]
    keys = jnp.concatenate([plain, ones_three((tokens, LANES))], axis=1)
    values = v_ref[0]
    spread = spread_ref[...]

    def scores(i):
        at = chunk_rows(i, chunk)
        s = dot_nt(jnp.concatenate([q_ref[0, at], aug_ref[0, at]], axis=1), keys)
        grad = dot_nn(m_ref[at], spread)
        delta = jnp.sum(grad * o_ref[0, at].astype(F32), axis=1, keepdims=True)
        return s, dot_nt(grad.astype(BF), values), delta

    def products(i, s, dp, delta):
        at = chunk_rows(i, chunk)
        ds = (jnp.exp2(s * (SCALE * LOG2E)) * (dp - delta)).astype(BF)
        dq_ref[at] = (dot_nn(ds, plain) * SCALE).astype(BF)
        return dot_tn(ds, q_ref[0, at])

    if count <= 4:
        ahead = scores(0)
        total = None
        for i in range(count):
            now = ahead
            if i + 1 < count:
                ahead = scores(i + 1)
            part = products(i, *now)
            total = part if total is None else total + part
        dk = (total * SCALE).astype(BF)
    else:
        dk_ref[...] = jnp.zeros(dk_ref.shape, F32)

        def step(i, carry):
            dk_ref[...] += products(i, *scores(i))
            return carry

        lax.fori_loop(0, count, step, 0)
        dk = (dk_ref[...] * SCALE).astype(BF)
    me = lax.axis_index("gen")
    for s in range(blocks):
        at = slice(s * LANES, (s + 1) * LANES)
        out_ref = out_refs[s] if apart else out_refs[0].at[me ^ s]
        out_ref[:LANES] = dq_ref[at]
        out_ref[LANES : 2 * LANES] = dk[at]
        out_ref[2 * LANES : 2 * LANES + FR] = spread[:FR]
        if apart:
            out_ref[2 * LANES + FR :] = extra_ref[...]


def received(blocks, near_refs, far_refs, s):
    near = len(near_refs)
    if s < near:
        return [near_refs[s]]
    return [far_refs[i + s - near] for i in range(0, len(far_refs), blocks - near)]


def value_columns(rows, spread):
    parts = [
        dot_tn(rows[:, at : at + HS], spread[:, at : at + HS]).astype(BF)
        for at in range(0, rows.shape[1], HS)
    ]
    return jnp.concatenate(parts, axis=1) if len(parts) > 1 else parts[0]


def settle_kernel(blocks, lw, first, near, far, *refs):
    near_refs, far_refs, refs = refs[:near], refs[near : near + far], refs[near + far :]
    if first:
        early_ref, latent_ref, rows_ref, dq_ref, dk_ref, dv_ref = refs
    else:
        latent_ref, rows_ref = refs
    me = lax.axis_index("gen")
    for s in range(blocks):
        d = me ^ s
        start = 0
        for ref in received(blocks, near_refs, far_refs, s):
            at = pl.ds(pl.multiple_of(d * lw + start, LANES), ref.shape[1])
            latent_ref[:, at] = ref[:LANES]
            start += ref.shape[1]
        rows = [ref[LANES:] for ref in received(blocks, near_refs, far_refs, s)]
        rows = jnp.concatenate(rows, axis=1) if len(rows) > 1 else rows[0]
        rows_ref[s] = rows[:, first:]
        if first:
            spread = early_ref[d, 2 * LANES :]
            at = pl.ds(pl.multiple_of(d * lw, LANES), first)
            dq_ref[:, at] = early_ref[d, :LANES]
            dk_ref[:, at] = early_ref[d, LANES : 2 * LANES]
            dv_ref[:, at] = value_columns(rows[:, :first], spread)


def finish_kernel(blocks, lw, chunk, *refs):
    late_refs, rows_ref = refs[:blocks], refs[blocks]
    dq_ref, dk_ref, dv_ref, heads_ref, made_ref, sems = refs[-6:]
    me = lax.axis_index("gen")
    last = rows_ref.shape[2]
    per = last // LANES
    copies = []
    for s in range(blocks):
        d = me ^ s
        late = late_refs[s]
        at = pl.ds(pl.multiple_of(d * lw + lw - last, LANES), last)
        made_ref[s] = value_columns(rows_ref[s], late[2 * LANES : 2 * LANES + FR])
        for source, out in (
            (late.at[:LANES], dq_ref),
            (late.at[LANES : 2 * LANES], dk_ref),
            (made_ref.at[s], dv_ref),
        ):
            copies.append(pltpu.make_async_copy(source, out.at[:, at], sems.at[len(copies)]))
            copies[-1].start()
        for piece in range(chunk // LANES):
            row = 2 * LANES + FR + piece // per * NDH
            lane = piece % per * LANES
            at = pl.ds(pl.multiple_of(d * chunk + piece * LANES, LANES), LANES)
            heads_ref[:, at] = late[row : row + NDH, lane : lane + LANES].astype(F32)
    for copy in copies:
        copy.wait()


def exchange(array):
    return lax.all_to_all(array, "gen", split_axis=0, concat_axis=0, tiled=True)


def on_device(
    query_in, key_in, value_in, teacher_w, disc_heads, frame_of_token, head_of_frame, timestep
):
    n = lax.axis_size("gen")
    grp = lax.axis_size("grp")
    me = lax.axis_index("gen")
    tok = query_in.shape[1]
    width = query_in.shape[2]
    tokens = tok * n
    heads = width // HS // n
    lw = heads * HS
    dh = teacher_w.shape[1]
    columns = dh // n
    chunk = -(-columns // LANES) * LANES
    rows = row_chunk(tokens)

    far, near = list(range(n // 2, n)), list(range(1, n // 2))
    half = len(far)

    def columns_for(array, s):
        return lax.dynamic_slice_in_dim(array, (me ^ s) * lw, lw, axis=1)

    def send(array, s):
        return lax.ppermute(array, "gen", [(i, i ^ s) for i in range(n)])

    def query_key(s):
        return jnp.stack([columns_for(query_in[0], s), columns_for(key_in[0], s)])

    qk, v = {0: query_key(0)}, {0: columns_for(value_in[0], 0)}
    blocks = {s: query_key(s) for s in far}
    for s in far:
        qk[s] = send(blocks[s], s)
    most = [qk[s] for s in far[: half - 1]]
    every = [qk[s] for s in far]
    for s in near:
        behind = [qk[s - 1]] if s > 1 else list(blocks.values())
        qk[s] = send(after(query_key(s), *behind), s)
    for s in near:
        behind = v[s - 1] if s > 1 else qk[s]
        v[s] = send(after(columns_for(value_in[0], s), behind), s)
    for i, s in enumerate(far):
        v[s] = send(after(columns_for(value_in[0], s), *(most if i < 2 else every)), s)
    qk, v = [qk[s] for s in range(n)], [v[s] for s in range(n)]

    frames = frame_of_token[0]
    frames = jnp.take(frames.reshape(n, tok), me ^ jnp.arange(n), axis=0).reshape(tokens)
    member = (frames[:, None] == lax.broadcasted_iota(jnp.int32, (tokens, LANES), 1)).astype(BF)
    member_t = (
        frames[None, :] == lax.broadcasted_iota(jnp.int32, (RR, tokens), 0)
    )
    counts = jnp.sum(member_t.astype(F32), axis=1)[:FR]
    member_t = jnp.transpose(
        member_t.astype(BF).reshape(RR, tokens // rows, rows), (1, 0, 2)
    )
    weight = (timestep[0].astype(F32) + 1.0) / NSTEPS
    lane = lax.broadcasted_iota(jnp.int32, (FR, LANES), 1)
    meta = jnp.where(lane == 0, counts[:, None], weight)
    head_ids = jnp.concatenate([head_of_frame[0], jnp.full((FR - FRAMES,), NDH, jnp.int32)])
    picked = (
        head_ids[:, None] == lax.broadcasted_iota(jnp.int32, (FR, NDH), 1)
    ).astype(F32)
    my_heads = lax.dynamic_slice_in_dim(disc_heads, me * columns, columns, axis=1)
    my_heads = jnp.pad(my_heads, ((0, 0), (0, chunk - columns)))
    head_rows = jnp.sum(picked[:, :, None] * my_heads[None], axis=1)
    if chunk == columns:
        w = teacher_w
    else:
        w = jnp.transpose(teacher_w.reshape(lw, n, columns), (1, 0, 2))
        w = jnp.pad(w, ((0, 0), (0, 0), (0, chunk - columns)))

    head_block = pl.BlockSpec((1, tokens, HS), lambda h: (h, 0, 0))
    head_shape = pltpu.HBM((heads, tokens, HS), BF)
    r_block = pl.BlockSpec((n, 1, FR, LANES), lambda h: (0, h, 0, 0))
    square = 2 * tokens * tokens * HS
    in_vmem = pl.BlockSpec(memory_space=pltpu.VMEM)
    anywhere = pl.BlockSpec(memory_space=pl.ANY)
    weights_scratch = [pltpu.VMEM((n, lw, chunk), BF), pltpu.SemaphoreType.DMA((n,))]

    with jax.named_scope("softmax_stats"):
        aug, r, q_rows, k_rows = pl.pallas_call(
            functools.partial(stats_kernel, n),
            grid=(heads,),
            in_specs=[pl.BlockSpec((2, LANES, HS), lambda h: (0, 0, h))] * n
            + [pl.BlockSpec((tokens // rows, RR, rows), lambda h: (0, 0, 0))],
            out_specs=[head_block, r_block, head_block, head_block],
            out_shape=[
                head_shape,
                pltpu.HBM((n, heads, FR, LANES), BF),
                head_shape,
                head_shape,
            ],
            compiler_params=params(tokens),
            cost_estimate=pl.CostEstimate(
                flops=heads * square, bytes_accessed=4 << 20, transcendentals=heads * tokens**2
            ),
        )(*map(hbm, qk), member_t)

    with jax.named_scope("pool_project"):
        part, pooled = pl.pallas_call(
            functools.partial(pool_kernel, n, heads, chunk),
            in_specs=[in_vmem] * (n + 2) + [anywhere],
            scratch_shapes=weights_scratch,
            out_shape=[
                jax.ShapeDtypeStruct((n, FR, chunk + LANES), BF),
                jax.ShapeDtypeStruct((FR, lw), F32),
            ],
            compiler_params=params(tokens, 0),
        )(*v, r, meta, hbm(w))

    got = exchange(part)

    split = heads // 2
    parts = [(0, split), (split, heads)] if split else [(0, heads)]

    def output(first, last, behind, before):
        at = pl.BlockSpec((1, tokens, HS), lambda h: (h + first, 0, 0))
        near_at = pl.BlockSpec((LANES + FR, HS), lambda h: (0, h + first))
        far_at = pl.BlockSpec((LANES + FR, HS), lambda h: (0, h))
        shared = [pltpu.HBM((LANES + FR, lw), BF)] * (n - half)
        inputs = list(map(hbm, v + [q_rows, k_rows, aug, after(r, behind)] + before))
        kept = list(range(n - half)) + [n, n + 1]
        with jax.named_scope("attention_output"):
            made = pl.pallas_call(
                functools.partial(output_kernel, n),
                grid=(last - first,),
                in_specs=[pl.BlockSpec((LANES, HS), lambda h: (0, h + first))] * n
                + [at] * 3
                + [pl.BlockSpec((n, 1, FR, LANES), lambda h: (0, h + first, 0, 0))]
                + [anywhere] * len(before),
                out_specs=[near_at] * (n - half) + [far_at] * half + [at] * 2,
                out_shape=shared
                + [pltpu.HBM((LANES + FR, (last - first) * HS), BF)] * half
                + [head_shape] * 2,
                input_output_aliases={n + 4 + i: kept[i] for i in range(len(before))},
                compiler_params=params(tokens),
                cost_estimate=pl.CostEstimate(
                    flops=2 * (last - first) * square,
                    bytes_accessed=(last - first) << 20,
                    transcendentals=(last - first) * tokens**2,
                ),
            )(*inputs)
        return made[: n - half], made[n - half : n], made[n:]

    mixed_near, made, own = output(*parts[0], part, [])
    got = after(got, own[1])
    mixed = [[send(made[i], s) for i, s in enumerate(far)]]

    with jax.named_scope("discriminator"):
        direction, feature, root = pl.pallas_call(
            functools.partial(middle_kernel, n, chunk, width),
            out_shape=[
                jax.ShapeDtypeStruct((n, FR, chunk + LANES), BF),
                jax.ShapeDtypeStruct((FR, chunk), F32),
                jax.ShapeDtypeStruct((FR, LANES), F32),
            ],
            compiler_params=params(tokens, 0),
        )(got, head_rows)

    got_back = exchange(after(direction, mixed[0][0]))
    got_back = after(got_back, *mixed[0][1:])
    if split:
        mixed_near, made, own = output(*parts[1], direction, list(mixed_near) + list(own))
        got_back = after(got_back, own[1])
        rest = made

    with jax.named_scope("pooled_gradient"):
        spread, head_part = pl.pallas_call(
            functools.partial(spread_kernel, n, chunk, width, tokens),
            in_specs=[in_vmem, anywhere] + [in_vmem] * 5,
            scratch_shapes=weights_scratch,
            out_shape=[
                jax.ShapeDtypeStruct((LANES, lw), BF),
                jax.ShapeDtypeStruct((NDH, chunk), F32),
            ],
            compiler_params=params(tokens, 0),
        )(got_back, hbm(w), pooled, meta, root, feature, picked)

    def back(first, last, apart, extra):
        part = (last - first) * HS
        if apart:
            block = (2 * LANES + FR + extra.shape[0], HS)
        else:
            block = (n, 2 * LANES + FR, HS)
        shape = block[:-1] + (part,)
        count = n if apart else 1
        at = pl.BlockSpec((1, tokens, HS), lambda h: (h + first, 0, 0))
        with jax.named_scope("attention_back"):
            return pl.pallas_call(
                functools.partial(back_kernel, n, apart),
                grid=(last - first,),
                in_specs=[at] * 5
                + [
                    pl.BlockSpec((tokens, LANES), lambda h: (0, 0)),
                    pl.BlockSpec((LANES, HS), lambda h: (0, h + first)),
                    pl.BlockSpec((extra.shape[0], HS), lambda h: (0, h)),
                ],
                out_specs=[pl.BlockSpec(block, lambda h: (0,) * (len(block) - 1) + (h,))] * count,
                out_shape=[pltpu.HBM(shape, BF)] * count,
                scratch_shapes=[pltpu.VMEM((tokens, HS), F32), pltpu.VMEM((tokens, HS), BF)],
                compiler_params=params(tokens),
                cost_estimate=pl.CostEstimate(
                    flops=4 * (last - first) * square,
                    bytes_accessed=(last - first) * (2 << 20),
                    transcendentals=(last - first) * tokens**2,
                ),
            )(*map(hbm, [q_rows, k_rows, *own, aug]), member, spread, extra)

    mixed_near = [mixed_near[0]] + [send(mixed_near[s], s) for s in near]
    if split:
        mixed.append([send(after(rest[i], spread), s) for i, s in enumerate(far)])
        spread = after(spread, mixed[1][0], *mixed_near[1:])
    head_sum = head_part
    if grp > 1:
        head_sum = head_sum + lax.ppermute(head_part, "grp", [(i, i ^ 1) for i in range(grp)])
    early = []
    first = split
    if first:
        made = back(0, first, False, jnp.zeros((NDH, first * HS), BF))[0]
        spread, head_sum, made = lax.optimization_barrier((spread, head_sum, made))
        early = [exchange(after(made, mixed[0][-1], *mixed[1]))]

    step = 2
    while step < grp:
        head_sum = head_sum + lax.ppermute(
            head_sum, "grp", [(i, i ^ step) for i in range(grp)]
        )
        step *= 2
    late_width = lw - first * HS
    groups = -(-chunk // late_width)
    extra = jnp.pad(head_sum.astype(BF), ((0, 0), (0, groups * late_width - chunk)))
    extra = jnp.transpose(extra.reshape(NDH, groups, late_width), (1, 0, 2))
    made = back(first, heads, True, extra.reshape(groups * NDH, late_width))
    late = [made[0]] + [send(made[s], s) for s in range(1, n)]

    whole = jax.ShapeDtypeStruct((tok, width), BF)
    far_blocks = [block for blocks in mixed for block in blocks]
    frame_rows = jax.ShapeDtypeStruct((n, FR, late_width), BF)
    with jax.named_scope("settle"):
        latents, frame_rows, *begun = pl.pallas_call(
            functools.partial(settle_kernel, n, lw, first * HS, n - half, len(far_blocks)),
            out_shape=[whole, frame_rows] + ([pltpu.HBM((tok, width), BF)] * 3 if first else []),
            compiler_params=params(tokens, 0),
        )(*map(hbm, mixed_near + far_blocks + early))
    late[0] = after(late[0], latents)
    with jax.named_scope("finish"):
        out_query, out_key, out_value, grad_heads = pl.pallas_call(
            functools.partial(finish_kernel, n, lw, chunk),
            in_specs=[in_vmem] * (n + 1) + [anywhere] * len(begun),
            out_specs=[anywhere] * 3 + [in_vmem],
            out_shape=[pltpu.HBM((tok, width), BF)] * 3
            + [jax.ShapeDtypeStruct((NDH, n * chunk), F32)],
            input_output_aliases={n + 1 + i: i for i in range(len(begun))},
            scratch_shapes=[
                pltpu.VMEM((n, LANES, late_width), BF),
                pltpu.SemaphoreType.DMA((3 * n,)),
            ],
            compiler_params=params(tokens, 0),
        )(*map(hbm, late), frame_rows, *map(hbm, begun))
    if chunk != columns:
        grad_heads = grad_heads.reshape(NDH, n, chunk)[:, :, :columns].reshape(NDH, dh)

    return (latents[None], out_query[None], out_key[None], out_value[None], grad_heads)


def solution(mesh):
    return jax.shard_map(
        on_device,
        mesh=mesh,
        in_specs=(
            P("grp", "gen", None),
            P("grp", "gen", None),
            P("grp", "gen", None),
            P("gen", None),
            P(),
            P("grp", None),
            P("grp", None),
            P("grp"),
        ),
        out_specs=(
            P("grp", "gen", None),
            P("grp", "gen", None),
            P("grp", "gen", None),
            P("grp", "gen", None),
            P(),
        ),
        check_vma=False,
    )
```

```python
import functools
import math

import jax
import jax.numpy as jnp
from jax import lax
from jax.experimental import pallas as pl
from jax.experimental.pallas import tpu as pltpu
from jax.sharding import PartitionSpec as P

HS = 128
FRAMES = 21
FR = 24
RR = 32
NDH = 8
NSTEPS = 1000
LANES = 128
epsilon = 1e-06
SCALE = 1.0 / math.sqrt(HS)
LOG2E = math.log2(math.e)
BF = jnp.bfloat16
F32 = jnp.float32


def params(tokens, axes=1):
    return pltpu.CompilerParams(
        vmem_limit_bytes=min(48, 16 * -(-tokens // 1024)) * 1024 * 1024,
        dimension_semantics=("arbitrary",) * axes,
    )


def hbm(array):
    return pltpu.with_memory_space_constraint(array, pltpu.HBM)


def after(value, *earlier):
    return lax.optimization_barrier((value,) + earlier)[0]


def dot_nn(a, b):
    return lax.dot_general(a, b, (((1,), (0,)), ((), ())), preferred_element_type=F32)


def dot_nt(a, b):
    return lax.dot_general(a, b, (((1,), (1,)), ((), ())), preferred_element_type=F32)


def dot_tn(a, b):
    return lax.dot_general(a, b, (((0,), (0,)), ((), ())), preferred_element_type=F32)


def rows_of(ref):
    block = ref[...]
    return block.reshape(block.shape[-3] * block.shape[-2], block.shape[-1])


def split_three(value):
    high = value.astype(BF)
    rest = value - high.astype(F32)
    middle = rest.astype(BF)
    low = (rest - middle.astype(F32)).astype(BF)
    return high, middle, low


def lanes_three(value, shape, first):
    lane = lax.broadcasted_iota(jnp.int32, shape, 1)
    out = jnp.zeros(shape, F32)
    for i, part in enumerate(split_three(value)):
        out = jnp.where(lane == first + i, part.astype(F32), out)
    return out


def ones_three(shape):
    lane = lax.broadcasted_iota(jnp.int32, shape, 1)
    return jnp.where(lane < 3, 1.0, 0.0).astype(BF)


def take_lanes(block, first, count):
    lane = lax.broadcasted_iota(jnp.int32, block.shape, 1)
    keep = (lane >= first) & (lane < first + count)
    return jnp.sum(jnp.where(keep, block, 0.0), axis=1, keepdims=True)


def row_chunk(tokens):
    return min(256, tokens)


def run_steps(count, step, carry):
    if count <= 4:
        for i in range(count):
            carry = step(i, carry)
        return carry
    return lax.fori_loop(0, count, step, carry)


def chunk_rows(i, chunk):
    return pl.ds(pl.multiple_of(i * chunk, chunk), chunk)


def stats_kernel(blocks, *refs):
    qk_refs, (mt_ref, aug_ref, r_ref, q_ref, k_ref) = refs[:blocks], refs[blocks:]
    tokens = blocks * LANES
    chunk = row_chunk(tokens)
    for s in range(blocks):
        at = slice(s * LANES, (s + 1) * LANES)
        q_ref[0, at] = qk_refs[s][0]
        k_ref[0, at] = qk_refs[s][1]
    keys = k_ref[0]

    def step(i, total_r):
        at = chunk_rows(i, chunk)
        s = dot_nt(q_ref[0, at], keys) * (SCALE * LOG2E)
        peak = jnp.max(s, axis=1, keepdims=True)
        e = jnp.exp2(s - peak)
        total = jnp.sum(e, axis=1, keepdims=True)
        p = (e * (1.0 / total)).astype(BF)
        lse = (peak + jnp.log2(total)) * (-1.0 / (SCALE * LOG2E))
        aug_ref[0, at] = lanes_three(lse, (chunk, LANES), 0).astype(BF)
        return total_r + dot_nn(mt_ref[i], p)

    r = run_steps(tokens // chunk, step, jnp.zeros((RR, tokens), F32))
    for s in range(blocks):
        r_ref[s, 0] = r[:FR, s * LANES : (s + 1) * LANES].astype(BF)


def pool_kernel(blocks, heads, chunk, *refs):
    v_hbm, refs = refs[:blocks], refs[blocks:]
    r_hbm, meta_ref, w_hbm, part_ref, pooled_ref, v_ref, r_ref, near_sems, w_ref, sems = refs
    fetches = [pltpu.make_async_copy(r_hbm, r_ref, near_sems.at[blocks])]
    for s in range(blocks):
        at = slice(s * LANES, (s + 1) * LANES)
        fetches.append(pltpu.make_async_copy(v_hbm[s], v_ref.at[at], near_sems.at[s]))
    for fetch in fetches:
        fetch.start()
    copies = start_weights(w_hbm, w_ref, sems, blocks, chunk)
    count = jnp.maximum(take_lanes(meta_ref[...], 0, 1), 1.0)
    for fetch in fetches:
        fetch.wait()
    columns = []
    for h in range(heads):
        r = jnp.concatenate([r_ref[s, h] for s in range(blocks)], axis=1)
        columns.append(dot_nn(r, v_ref[:, h * HS : (h + 1) * HS]))
    pooled = jnp.concatenate(columns, axis=1) if heads > 1 else columns[0]
    pooled = pooled / count
    pooled_ref[...] = pooled
    squares = jnp.sum(pooled * pooled, axis=1, keepdims=True)
    stats = lanes_three(squares, (FR, LANES), 0).astype(BF)
    rounded = pooled.astype(BF)
    for d in range(blocks):
        copies[d].wait()
        part_ref[d, :, :chunk] = dot_nn(rounded, w_ref[d]).astype(BF)
        part_ref[d, :, chunk:] = stats


def start_weights(w_hbm, w_ref, sems, blocks, chunk):
    copies = []
    for d in range(blocks):
        if len(w_hbm.shape) == 3:
            source = w_hbm.at[d]
        else:
            source = w_hbm.at[:, d * chunk : (d + 1) * chunk]
        copies.append(pltpu.make_async_copy(source, w_ref.at[d], sems.at[d]))
        copies[d].start()
    return copies


def middle_kernel(blocks, chunk, width, got_ref, rows_ref, send_ref, feature_ref, root_ref):
    total = got_ref[0].astype(F32)
    for d in range(1, blocks):
        total = total + got_ref[d].astype(F32)
    projected = total[:, :chunk]
    squares = take_lanes(total[:, chunk:], 0, 3)
    root = jnp.sqrt(squares / width + epsilon)
    pre = projected / root
    gate = jax.nn.sigmoid(pre)
    feature = pre * gate
    head_rows = rows_ref[...]
    direction = head_rows * gate * (1.0 + pre * (1.0 - gate))
    score = jnp.sum(feature * head_rows, axis=1, keepdims=True)
    slope = jnp.sum(direction * pre, axis=1, keepdims=True)
    stats = (
        lanes_three(score, (FR, LANES), 0) + lanes_three(slope, (FR, LANES), 3)
    ).astype(BF)
    rounded = direction.astype(BF)
    for d in range(blocks):
        send_ref[d, :, :chunk] = rounded
        send_ref[d, :, chunk:] = stats
    feature_ref[...] = feature
    root_ref[...] = jnp.broadcast_to(root, (FR, LANES))


def spread_kernel(
    blocks,
    chunk,
    width,
    tokens,
    got_ref,
    w_hbm,
    pooled_ref,
    meta_ref,
    root_ref,
    feature_ref,
    picked_ref,
    spread_ref,
    heads_ref,
    w_ref,
    sems,
):
    copies = start_weights(w_hbm, w_ref, sems, blocks, chunk)
    meta = meta_ref[...]
    count = jnp.maximum(take_lanes(meta, 0, 1), 1.0)
    weight = take_lanes(meta, 1, 1)
    root = take_lanes(root_ref[...], 0, 1)
    stats = got_ref[0, :, chunk:].astype(F32)
    for d in range(1, blocks):
        stats = stats + got_ref[d, :, chunk:].astype(F32)
    score = take_lanes(stats, 0, 3)
    slope = take_lanes(stats, 3, 3)
    grad_score = -weight * jax.nn.sigmoid(-score) / FRAMES
    total = jnp.zeros(pooled_ref.shape, F32)
    for d in range(blocks):
        copies[d].wait()
        total = total + dot_nt(got_ref[d, :, :chunk], w_ref[d])
    grad_root = -(grad_score * slope) / root
    grad_pooled = (grad_score / root) * total + (grad_root / root / width) * pooled_ref[...]
    spread_ref[:FR] = (tokens * (grad_pooled / count)).astype(BF)
    spread_ref[FR:] = jnp.zeros((LANES - FR, pooled_ref.shape[1]), BF)
    scaled = feature_ref[...] * grad_score
    picked = picked_ref[...]
    for j in range(NDH):
        heads_ref[j : j + 1, :] = jnp.sum(scaled * picked[:, j : j + 1], axis=0, keepdims=True)


def output_kernel(blocks, *refs):
    v_refs, (q_ref, k_ref, aug_ref, r_ref) = refs[:blocks], refs[blocks : blocks + 4]
    send_refs, (v_ref, o_ref) = refs[-2 - blocks : -2], refs[-2:]
    tokens = blocks * LANES
    chunk = row_chunk(tokens)
    for s in range(blocks):
        v_ref[0, s * LANES : (s + 1) * LANES] = v_refs[s][...]
    keys = jnp.concatenate([k_ref[0], ones_three((tokens, LANES))], axis=1)
    values = v_ref[0]

    def step(i, carry):
        at = chunk_rows(i, chunk)
        s = dot_nt(jnp.concatenate([q_ref[0, at], aug_ref[0, at]], axis=1), keys)
        p = jnp.exp2(s * (SCALE * LOG2E)).astype(BF)
        o_ref[0, at] = dot_nn(p, values).astype(BF)
        return carry

    run_steps(tokens // chunk, step, 0)
    for s in range(blocks):
        send_refs[s][:LANES] = o_ref[0, s * LANES : (s + 1) * LANES]
        send_refs[s][LANES:] = r_ref[s, 0]


def back_kernel(
    blocks, apart, q_ref, k_ref, v_ref, o_ref, aug_ref, m_ref, spread_ref, extra_ref, *refs
):
    out_refs, dk_ref, dq_ref = refs[:-2], refs[-2], refs[-1]
    tokens = blocks * LANES
    chunk = row_chunk(tokens)
    count = tokens // chunk
    plain = k_ref[0]
    keys = jnp.concatenate([plain, ones_three((tokens, LANES))], axis=1)
    values = v_ref[0]
    spread = spread_ref[...]

    def scores(i):
        at = chunk_rows(i, chunk)
        s = dot_nt(jnp.concatenate([q_ref[0, at], aug_ref[0, at]], axis=1), keys)
        grad = dot_nn(m_ref[at], spread)
        delta = jnp.sum(grad * o_ref[0, at].astype(F32), axis=1, keepdims=True)
        return s, dot_nt(grad.astype(BF), values), delta

    def products(i, s, dp, delta):
        at = chunk_rows(i, chunk)
        ds = (jnp.exp2(s * (SCALE * LOG2E)) * (dp - delta)).astype(BF)
        dq_ref[at] = (dot_nn(ds, plain) * SCALE).astype(BF)
        return dot_tn(ds, q_ref[0, at])

    if count <= 4:
        ahead = scores(0)
        total = None
        for i in range(count):
            now = ahead
            if i + 1 < count:
                ahead = scores(i + 1)
            part = products(i, *now)
            total = part if total is None else total + part
        dk = (total * SCALE).astype(BF)
    else:
        dk_ref[...] = jnp.zeros(dk_ref.shape, F32)

        def step(i, carry):
            dk_ref[...] += products(i, *scores(i))
            return carry

        lax.fori_loop(0, count, step, 0)
        dk = (dk_ref[...] * SCALE).astype(BF)
    me = lax.axis_index("gen")
    for s in range(blocks):
        at = slice(s * LANES, (s + 1) * LANES)
        out_ref = out_refs[s] if apart else out_refs[0].at[me ^ s]
        out_ref[:LANES] = dq_ref[at]
        out_ref[LANES : 2 * LANES] = dk[at]
        out_ref[2 * LANES : 2 * LANES + FR] = spread[:FR]
        if apart:
            out_ref[2 * LANES + FR :] = extra_ref[...]


def received(blocks, near_refs, far_refs, s):
    near = len(near_refs)
    if s < near:
        return [near_refs[s]]
    return [far_refs[i + s - near] for i in range(0, len(far_refs), blocks - near)]


def value_columns(rows, spread):
    parts = [
        dot_tn(rows[:, at : at + HS], spread[:, at : at + HS]).astype(BF)
        for at in range(0, rows.shape[1], HS)
    ]
    return jnp.concatenate(parts, axis=1) if len(parts) > 1 else parts[0]


def settle_kernel(blocks, lw, first, near, far, *refs):
    near_refs, far_refs, refs = refs[:near], refs[near : near + far], refs[near + far :]
    if first:
        early_ref, latent_ref, rows_ref, dq_ref, dk_ref, dv_ref = refs
    else:
        latent_ref, rows_ref = refs
    me = lax.axis_index("gen")
    for s in range(blocks):
        d = me ^ s
        start = 0
        for ref in received(blocks, near_refs, far_refs, s):
            at = pl.ds(pl.multiple_of(d * lw + start, LANES), ref.shape[1])
            latent_ref[:, at] = ref[:LANES]
            start += ref.shape[1]
        rows = [ref[LANES:] for ref in received(blocks, near_refs, far_refs, s)]
        rows = jnp.concatenate(rows, axis=1) if len(rows) > 1 else rows[0]
        rows_ref[s] = rows[:, first:]
        if first:
            spread = early_ref[d, 2 * LANES :]
            at = pl.ds(pl.multiple_of(d * lw, LANES), first)
            dq_ref[:, at] = early_ref[d, :LANES]
            dk_ref[:, at] = early_ref[d, LANES : 2 * LANES]
            dv_ref[:, at] = value_columns(rows[:, :first], spread)


def finish_kernel(blocks, lw, chunk, *refs):
    late_refs, rows_ref = refs[:blocks], refs[blocks]
    dq_ref, dk_ref, dv_ref, heads_ref, made_ref, sems = refs[-6:]
    me = lax.axis_index("gen")
    last = rows_ref.shape[2]
    per = last // LANES
    copies = []
    for s in range(blocks):
        d = me ^ s
        late = late_refs[s]
        at = pl.ds(pl.multiple_of(d * lw + lw - last, LANES), last)
        made_ref[s] = value_columns(rows_ref[s], late[2 * LANES : 2 * LANES + FR])
        for source, out in (
            (late.at[:LANES], dq_ref),
            (late.at[LANES : 2 * LANES], dk_ref),
            (made_ref.at[s], dv_ref),
        ):
            copies.append(pltpu.make_async_copy(source, out.at[:, at], sems.at[len(copies)]))
            copies[-1].start()
        for piece in range(chunk // LANES):
            row = 2 * LANES + FR + piece // per * NDH
            lane = piece % per * LANES
            at = pl.ds(pl.multiple_of(d * chunk + piece * LANES, LANES), LANES)
            heads_ref[:, at] = late[row : row + NDH, lane : lane + LANES].astype(F32)
    for copy in copies:
        copy.wait()


def exchange(array):
    return lax.all_to_all(array, "gen", split_axis=0, concat_axis=0, tiled=True)


def on_device(
    query_in, key_in, value_in, teacher_w, disc_heads, frame_of_token, head_of_frame, timestep
):
    n = lax.axis_size("gen")
    grp = lax.axis_size("grp")
    me = lax.axis_index("gen")
    tok = query_in.shape[1]
    width = query_in.shape[2]
    tokens = tok * n
    heads = width // HS // n
    lw = heads * HS
    dh = teacher_w.shape[1]
    columns = dh // n
    chunk = -(-columns // LANES) * LANES
    rows = row_chunk(tokens)

    far, near = list(range(n // 2, n)), list(range(1, n // 2))
    half = len(far)

    def columns_for(array, s):
        return lax.dynamic_slice_in_dim(array, (me ^ s) * lw, lw, axis=1)

    def send(array, s):
        return lax.ppermute(array, "gen", [(i, i ^ s) for i in range(n)])

    def query_key(s):
        return jnp.stack([columns_for(query_in[0], s), columns_for(key_in[0], s)])

    qk, v = {0: query_key(0)}, {0: columns_for(value_in[0], 0)}
    blocks = {s: query_key(s) for s in far}
    for s in far:
        qk[s] = send(blocks[s], s)
    most = [qk[s] for s in far[: half - 1]]
    every = [qk[s] for s in far]
    for s in near:
        behind = [qk[s - 1]] if s > 1 else list(blocks.values())
        qk[s] = send(after(query_key(s), *behind), s)
    for s in near:
        behind = v[s - 1] if s > 1 else qk[s]
        v[s] = send(after(columns_for(value_in[0], s), behind), s)
    for i, s in enumerate(far):
        v[s] = send(after(columns_for(value_in[0], s), *(most if i < 2 else every)), s)
    qk, v = [qk[s] for s in range(n)], [v[s] for s in range(n)]

    frames = frame_of_token[0]
    frames = jnp.take(frames.reshape(n, tok), me ^ jnp.arange(n), axis=0).reshape(tokens)
    member = (frames[:, None] == lax.broadcasted_iota(jnp.int32, (tokens, LANES), 1)).astype(BF)
    member_t = (
        frames[None, :] == lax.broadcasted_iota(jnp.int32, (RR, tokens), 0)
    )
    counts = jnp.sum(member_t.astype(F32), axis=1)[:FR]
    member_t = jnp.transpose(
        member_t.astype(BF).reshape(RR, tokens // rows, rows), (1, 0, 2)
    )
    weight = (timestep[0].astype(F32) + 1.0) / NSTEPS
    lane = lax.broadcasted_iota(jnp.int32, (FR, LANES), 1)
    meta = jnp.where(lane == 0, counts[:, None], weight)
    head_ids = jnp.concatenate([head_of_frame[0], jnp.full((FR - FRAMES,), NDH, jnp.int32)])
    picked = (
        head_ids[:, None] == lax.broadcasted_iota(jnp.int32, (FR, NDH), 1)
    ).astype(F32)
    my_heads = lax.dynamic_slice_in_dim(disc_heads, me * columns, columns, axis=1)
    my_heads = jnp.pad(my_heads, ((0, 0), (0, chunk - columns)))
    head_rows = jnp.sum(picked[:, :, None] * my_heads[None], axis=1)
    if chunk == columns:
        w = teacher_w
    else:
        w = jnp.transpose(teacher_w.reshape(lw, n, columns), (1, 0, 2))
        w = jnp.pad(w, ((0, 0), (0, 0), (0, chunk - columns)))

    head_block = pl.BlockSpec((1, tokens, HS), lambda h: (h, 0, 0))
    head_shape = pltpu.HBM((heads, tokens, HS), BF)
    r_block = pl.BlockSpec((n, 1, FR, LANES), lambda h: (0, h, 0, 0))
    square = 2 * tokens * tokens * HS
    in_vmem = pl.BlockSpec(memory_space=pltpu.VMEM)
    anywhere = pl.BlockSpec(memory_space=pl.ANY)
    weights_scratch = [pltpu.VMEM((n, lw, chunk), BF), pltpu.SemaphoreType.DMA((n,))]

    with jax.named_scope("softmax_stats"):
        aug, r, q_rows, k_rows = pl.pallas_call(
            functools.partial(stats_kernel, n),
            grid=(heads,),
            in_specs=[pl.BlockSpec((2, LANES, HS), lambda h: (0, 0, h))] * n
            + [pl.BlockSpec((tokens // rows, RR, rows), lambda h: (0, 0, 0))],
            out_specs=[head_block, r_block, head_block, head_block],
            out_shape=[
                head_shape,
                pltpu.HBM((n, heads, FR, LANES), BF),
                head_shape,
                head_shape,
            ],
            compiler_params=params(tokens),
            cost_estimate=pl.CostEstimate(
                flops=heads * square, bytes_accessed=4 << 20, transcendentals=heads * tokens**2
            ),
        )(*map(hbm, qk), member_t)

    with jax.named_scope("pool_project"):
        part, pooled = pl.pallas_call(
            functools.partial(pool_kernel, n, heads, chunk),
            in_specs=[anywhere] * (n + 1) + [in_vmem, anywhere],
            scratch_shapes=[
                pltpu.VMEM((tokens, lw), BF),
                pltpu.VMEM((n, heads, FR, LANES), BF),
                pltpu.SemaphoreType.DMA((n + 1,)),
            ]
            + weights_scratch,
            out_shape=[
                jax.ShapeDtypeStruct((n, FR, chunk + LANES), BF),
                jax.ShapeDtypeStruct((FR, lw), F32),
            ],
            compiler_params=params(tokens, 0),
        )(*v, hbm(r), meta, hbm(w))

    got = exchange(part)

    split = heads // 2
    parts = [(0, split), (split, heads)] if split else [(0, heads)]

    def output(first, last, behind, before):
        at = pl.BlockSpec((1, tokens, HS), lambda h: (h + first, 0, 0))
        near_at = pl.BlockSpec((LANES + FR, HS), lambda h: (0, h + first))
        far_at = pl.BlockSpec((LANES + FR, HS), lambda h: (0, h))
        shared = [pltpu.HBM((LANES + FR, lw), BF)] * (n - half)
        inputs = list(map(hbm, v + [q_rows, k_rows, aug, after(r, behind)] + before))
        kept = list(range(n - half)) + [n, n + 1]
        with jax.named_scope("attention_output"):
            made = pl.pallas_call(
                functools.partial(output_kernel, n),
                grid=(last - first,),
                in_specs=[pl.BlockSpec((LANES, HS), lambda h: (0, h + first))] * n
                + [at] * 3
                + [pl.BlockSpec((n, 1, FR, LANES), lambda h: (0, h + first, 0, 0))]
                + [anywhere] * len(before),
                out_specs=[near_at] * (n - half) + [far_at] * half + [at] * 2,
                out_shape=shared
                + [pltpu.HBM((LANES + FR, (last - first) * HS), BF)] * half
                + [head_shape] * 2,
                input_output_aliases={n + 4 + i: kept[i] for i in range(len(before))},
                compiler_params=params(tokens),
                cost_estimate=pl.CostEstimate(
                    flops=2 * (last - first) * square,
                    bytes_accessed=(last - first) << 20,
                    transcendentals=(last - first) * tokens**2,
                ),
            )(*inputs)
        return made[: n - half], made[n - half : n], made[n:]

    mixed_near, made, own = output(*parts[0], part, [])
    got = after(got, own[1])
    mixed = [[send(made[i], s) for i, s in enumerate(far)]]

    with jax.named_scope("discriminator"):
        direction, feature, root = pl.pallas_call(
            functools.partial(middle_kernel, n, chunk, width),
            out_shape=[
                jax.ShapeDtypeStruct((n, FR, chunk + LANES), BF),
                jax.ShapeDtypeStruct((FR, chunk), F32),
                jax.ShapeDtypeStruct((FR, LANES), F32),
            ],
            compiler_params=params(tokens, 0),
        )(got, head_rows)

    got_back = exchange(after(direction, mixed[0][0]))
    got_back = after(got_back, *mixed[0][1:])
    if split:
        mixed_near, made, own = output(*parts[1], direction, list(mixed_near) + list(own))
        got_back = after(got_back, own[1])
        rest = made

    with jax.named_scope("pooled_gradient"):
        spread, head_part = pl.pallas_call(
            functools.partial(spread_kernel, n, chunk, width, tokens),
            in_specs=[in_vmem, anywhere] + [in_vmem] * 5,
            scratch_shapes=weights_scratch,
            out_shape=[
                jax.ShapeDtypeStruct((LANES, lw), BF),
                jax.ShapeDtypeStruct((NDH, chunk), F32),
            ],
            compiler_params=params(tokens, 0),
        )(got_back, hbm(w), pooled, meta, root, feature, picked)

    def back(first, last, apart, extra):
        part = (last - first) * HS
        if apart:
            block = (2 * LANES + FR + extra.shape[0], HS)
        else:
            block = (n, 2 * LANES + FR, HS)
        shape = block[:-1] + (part,)
        count = n if apart else 1
        at = pl.BlockSpec((1, tokens, HS), lambda h: (h + first, 0, 0))
        with jax.named_scope("attention_back"):
            return pl.pallas_call(
                functools.partial(back_kernel, n, apart),
                grid=(last - first,),
                in_specs=[at] * 5
                + [
                    pl.BlockSpec((tokens, LANES), lambda h: (0, 0)),
                    pl.BlockSpec((LANES, HS), lambda h: (0, h + first)),
                    pl.BlockSpec((extra.shape[0], HS), lambda h: (0, h)),
                ],
                out_specs=[pl.BlockSpec(block, lambda h: (0,) * (len(block) - 1) + (h,))] * count,
                out_shape=[pltpu.HBM(shape, BF)] * count,
                scratch_shapes=[pltpu.VMEM((tokens, HS), F32), pltpu.VMEM((tokens, HS), BF)],
                compiler_params=params(tokens),
                cost_estimate=pl.CostEstimate(
                    flops=4 * (last - first) * square,
                    bytes_accessed=(last - first) * (2 << 20),
                    transcendentals=(last - first) * tokens**2,
                ),
            )(*map(hbm, [q_rows, k_rows, *own, aug]), member, spread, extra)

    mixed_near = [mixed_near[0]] + [send(mixed_near[s], s) for s in near]
    if split:
        mixed.append([send(after(rest[i], spread), s) for i, s in enumerate(far)])
        spread = after(spread, mixed[1][0], *mixed_near[1:])
    head_sum = head_part
    if grp > 1:
        head_sum = head_sum + lax.ppermute(head_part, "grp", [(i, i ^ 1) for i in range(grp)])
    early = []
    first = split
    if first:
        made = back(0, first, False, jnp.zeros((NDH, first * HS), BF))[0]
        spread, head_sum, made = lax.optimization_barrier((spread, head_sum, made))
        early = [exchange(after(made, mixed[0][-1], *mixed[1]))]

    step = 2
    while step < grp:
        head_sum = head_sum + lax.ppermute(
            head_sum, "grp", [(i, i ^ step) for i in range(grp)]
        )
        step *= 2
    late_width = lw - first * HS
    groups = -(-chunk // late_width)
    extra = jnp.pad(head_sum.astype(BF), ((0, 0), (0, groups * late_width - chunk)))
    extra = jnp.transpose(extra.reshape(NDH, groups, late_width), (1, 0, 2))
    made = back(first, heads, True, extra.reshape(groups * NDH, late_width))
    late = [made[0]] + [send(made[s], s) for s in range(1, n)]

    whole = jax.ShapeDtypeStruct((tok, width), BF)
    far_blocks = [block for blocks in mixed for block in blocks]
    frame_rows = jax.ShapeDtypeStruct((n, FR, late_width), BF)
    with jax.named_scope("settle"):
        latents, frame_rows, *begun = pl.pallas_call(
            functools.partial(settle_kernel, n, lw, first * HS, n - half, len(far_blocks)),
            out_shape=[whole, frame_rows] + ([pltpu.HBM((tok, width), BF)] * 3 if first else []),
            compiler_params=params(tokens, 0),
        )(*mixed_near, *far_blocks, *map(hbm, early))
    late[0] = after(late[0], latents)
    with jax.named_scope("finish"):
        out_query, out_key, out_value, grad_heads = pl.pallas_call(
            functools.partial(finish_kernel, n, lw, chunk),
            in_specs=[in_vmem] * (n + 1) + [anywhere] * len(begun),
            out_specs=[anywhere] * 3 + [in_vmem],
            out_shape=[pltpu.HBM((tok, width), BF)] * 3
            + [jax.ShapeDtypeStruct((NDH, n * chunk), F32)],
            input_output_aliases={n + 1 + i: i for i in range(len(begun))},
            scratch_shapes=[
                pltpu.VMEM((n, LANES, late_width), BF),
                pltpu.SemaphoreType.DMA((3 * n,)),
            ],
            compiler_params=params(tokens, 0),
        )(*late, frame_rows, *map(hbm, begun))
    if chunk != columns:
        grad_heads = grad_heads.reshape(NDH, n, chunk)[:, :, :columns].reshape(NDH, dh)

    return (latents[None], out_query[None], out_key[None], out_value[None], grad_heads)


def solution(mesh):
    return jax.shard_map(
        on_device,
        mesh=mesh,
        in_specs=(
            P("grp", "gen", None),
            P("grp", "gen", None),
            P("grp", "gen", None),
            P("gen", None),
            P(),
            P("grp", None),
            P("grp", None),
            P("grp"),
        ),
        out_specs=(
            P("grp", "gen", None),
            P("grp", "gen", None),
            P("grp", "gen", None),
            P("grp", "gen", None),
            P(),
        ),
        check_vma=False,
    )
```

```python
import functools
import math

import jax
import jax.numpy as jnp
from jax import lax
from jax.experimental import pallas as pl
from jax.experimental.pallas import tpu as pltpu
from jax.sharding import PartitionSpec as P

HS = 128
FRAMES = 21
FR = 24
RR = 32
NDH = 8
NSTEPS = 1000
LANES = 128
epsilon = 1e-06
SCALE = 1.0 / math.sqrt(HS)
LOG2E = math.log2(math.e)
BF = jnp.bfloat16
F32 = jnp.float32


def params(tokens, axes=1):
    return pltpu.CompilerParams(
        vmem_limit_bytes=min(48, 16 * -(-tokens // 1024)) * 1024 * 1024,
        dimension_semantics=("arbitrary",) * axes,
    )


def hbm(array):
    return pltpu.with_memory_space_constraint(array, pltpu.HBM)


def after(value, *earlier):
    return lax.optimization_barrier((value,) + earlier)[0]


def dot_nn(a, b):
    return lax.dot_general(a, b, (((1,), (0,)), ((), ())), preferred_element_type=F32)


def dot_nt(a, b):
    return lax.dot_general(a, b, (((1,), (1,)), ((), ())), preferred_element_type=F32)


def dot_tn(a, b):
    return lax.dot_general(a, b, (((0,), (0,)), ((), ())), preferred_element_type=F32)


def rows_of(ref):
    block = ref[...]
    return block.reshape(block.shape[-3] * block.shape[-2], block.shape[-1])


def split_three(value):
    high = value.astype(BF)
    rest = value - high.astype(F32)
    middle = rest.astype(BF)
    low = (rest - middle.astype(F32)).astype(BF)
    return high, middle, low


def lanes_three(value, shape, first):
    lane = lax.broadcasted_iota(jnp.int32, shape, 1)
    out = jnp.zeros(shape, F32)
    for i, part in enumerate(split_three(value)):
        out = jnp.where(lane == first + i, part.astype(F32), out)
    return out


def ones_three(shape):
    lane = lax.broadcasted_iota(jnp.int32, shape, 1)
    return jnp.where(lane < 3, 1.0, 0.0).astype(BF)


def take_lanes(block, first, count):
    lane = lax.broadcasted_iota(jnp.int32, block.shape, 1)
    keep = (lane >= first) & (lane < first + count)
    return jnp.sum(jnp.where(keep, block, 0.0), axis=1, keepdims=True)


def row_chunk(tokens):
    return min(256, tokens)


def run_steps(count, step, carry):
    if count <= 4:
        for i in range(count):
            carry = step(i, carry)
        return carry
    return lax.fori_loop(0, count, step, carry)


def chunk_rows(i, chunk):
    return pl.ds(pl.multiple_of(i * chunk, chunk), chunk)


def stats_kernel(blocks, *refs):
    qk_refs, (mt_ref, aug_ref, r_ref, q_ref, k_ref) = refs[:blocks], refs[blocks:]
    tokens = blocks * LANES
    chunk = row_chunk(tokens)
    for s in range(blocks):
        at = slice(s * LANES, (s + 1) * LANES)
        q_ref[0, at] = qk_refs[s][0]
        k_ref[0, at] = qk_refs[s][1]
    keys = k_ref[0]
    count = tokens // chunk

    def scores(i):
        return dot_nt(q_ref[0, chunk_rows(i, chunk)], keys)

    def reduce(i, raw):
        s = raw * (SCALE * LOG2E)
        peak = jnp.max(s, axis=1, keepdims=True)
        e = jnp.exp2(s - peak)
        total = jnp.sum(e, axis=1, keepdims=True)
        p = (e * (1.0 / total)).astype(BF)
        lse = (peak + jnp.log2(total)) * (-1.0 / (SCALE * LOG2E))
        aug_ref[0, chunk_rows(i, chunk)] = lanes_three(lse, (chunk, LANES), 0).astype(BF)
        return dot_nn(mt_ref[i], p)

    if count <= 4:
        ahead = scores(0)
        r = None
        for i in range(count):
            now = ahead
            if i + 1 < count:
                ahead = scores(i + 1)
            part = reduce(i, now)
            r = part if r is None else r + part
    else:
        r = lax.fori_loop(
            0, count, lambda i, r: r + reduce(i, scores(i)), jnp.zeros((RR, tokens), F32)
        )
    for s in range(blocks):
        r_ref[s, 0] = r[:FR, s * LANES : (s + 1) * LANES].astype(BF)


def pool_kernel(blocks, heads, chunk, *refs):
    v_hbm, refs = refs[:blocks], refs[blocks:]
    r_hbm, meta_ref, w_hbm, part_ref, pooled_ref, v_ref, r_ref, near_sems, w_ref, sems = refs
    fetches = [pltpu.make_async_copy(r_hbm, r_ref, near_sems.at[blocks])]
    for s in range(blocks):
        at = slice(s * LANES, (s + 1) * LANES)
        fetches.append(pltpu.make_async_copy(v_hbm[s], v_ref.at[at], near_sems.at[s]))
    for fetch in fetches:
        fetch.start()
    copies = start_weights(w_hbm, w_ref, sems, blocks, chunk)
    count = jnp.maximum(take_lanes(meta_ref[...], 0, 1), 1.0)
    for fetch in fetches:
        fetch.wait()
    columns = []
    for h in range(heads):
        r = jnp.concatenate([r_ref[s, h] for s in range(blocks)], axis=1)
        columns.append(dot_nn(r, v_ref[:, h * HS : (h + 1) * HS]))
    pooled = jnp.concatenate(columns, axis=1) if heads > 1 else columns[0]
    pooled = pooled / count
    pooled_ref[...] = pooled
    squares = jnp.sum(pooled * pooled, axis=1, keepdims=True)
    stats = lanes_three(squares, (FR, LANES), 0).astype(BF)
    rounded = pooled.astype(BF)
    for d in range(blocks):
        copies[d].wait()
        part_ref[d, :, :chunk] = dot_nn(rounded, w_ref[d]).astype(BF)
        part_ref[d, :, chunk:] = stats


def start_weights(w_hbm, w_ref, sems, blocks, chunk):
    copies = []
    for d in range(blocks):
        if len(w_hbm.shape) == 3:
            source = w_hbm.at[d]
        else:
            source = w_hbm.at[:, d * chunk : (d + 1) * chunk]
        copies.append(pltpu.make_async_copy(source, w_ref.at[d], sems.at[d]))
        copies[d].start()
    return copies


def middle_kernel(blocks, chunk, width, got_ref, rows_ref, send_ref, feature_ref, root_ref):
    total = got_ref[0].astype(F32)
    for d in range(1, blocks):
        total = total + got_ref[d].astype(F32)
    projected = total[:, :chunk]
    squares = take_lanes(total[:, chunk:], 0, 3)
    root = jnp.sqrt(squares / width + epsilon)
    pre = projected / root
    gate = jax.nn.sigmoid(pre)
    feature = pre * gate
    head_rows = rows_ref[...]
    direction = head_rows * gate * (1.0 + pre * (1.0 - gate))
    score = jnp.sum(feature * head_rows, axis=1, keepdims=True)
    slope = jnp.sum(direction * pre, axis=1, keepdims=True)
    stats = (
        lanes_three(score, (FR, LANES), 0) + lanes_three(slope, (FR, LANES), 3)
    ).astype(BF)
    rounded = direction.astype(BF)
    for d in range(blocks):
        send_ref[d, :, :chunk] = rounded
        send_ref[d, :, chunk:] = stats
    feature_ref[...] = feature
    root_ref[...] = jnp.broadcast_to(root, (FR, LANES))


def spread_kernel(
    blocks,
    chunk,
    width,
    tokens,
    got_ref,
    w_hbm,
    pooled_ref,
    meta_ref,
    root_ref,
    feature_ref,
    picked_ref,
    spread_ref,
    heads_ref,
    w_ref,
    sems,
):
    copies = start_weights(w_hbm, w_ref, sems, blocks, chunk)
    meta = meta_ref[...]
    count = jnp.maximum(take_lanes(meta, 0, 1), 1.0)
    weight = take_lanes(meta, 1, 1)
    root = take_lanes(root_ref[...], 0, 1)
    stats = got_ref[0, :, chunk:].astype(F32)
    for d in range(1, blocks):
        stats = stats + got_ref[d, :, chunk:].astype(F32)
    score = take_lanes(stats, 0, 3)
    slope = take_lanes(stats, 3, 3)
    grad_score = -weight * jax.nn.sigmoid(-score) / FRAMES
    total = jnp.zeros(pooled_ref.shape, F32)
    for d in range(blocks):
        copies[d].wait()
        total = total + dot_nt(got_ref[d, :, :chunk], w_ref[d])
    grad_root = -(grad_score * slope) / root
    grad_pooled = (grad_score / root) * total + (grad_root / root / width) * pooled_ref[...]
    spread_ref[:FR] = (tokens * (grad_pooled / count)).astype(BF)
    spread_ref[FR:] = jnp.zeros((LANES - FR, pooled_ref.shape[1]), BF)
    scaled = feature_ref[...] * grad_score
    picked = picked_ref[...]
    for j in range(NDH):
        heads_ref[j : j + 1, :] = jnp.sum(scaled * picked[:, j : j + 1], axis=0, keepdims=True)


def output_kernel(blocks, *refs):
    v_refs, (q_ref, k_ref, aug_ref, r_ref) = refs[:blocks], refs[blocks : blocks + 4]
    send_refs, (v_ref, o_ref) = refs[-2 - blocks : -2], refs[-2:]
    tokens = blocks * LANES
    chunk = row_chunk(tokens)
    for s in range(blocks):
        v_ref[0, s * LANES : (s + 1) * LANES] = v_refs[s][...]
    keys = jnp.concatenate([k_ref[0], ones_three((tokens, LANES))], axis=1)
    values = v_ref[0]

    def step(i, carry):
        at = chunk_rows(i, chunk)
        s = dot_nt(jnp.concatenate([q_ref[0, at], aug_ref[0, at]], axis=1), keys)
        p = jnp.exp2(s * (SCALE * LOG2E)).astype(BF)
        o_ref[0, at] = dot_nn(p, values).astype(BF)
        return carry

    run_steps(tokens // chunk, step, 0)
    for s in range(blocks):
        send_refs[s][:LANES] = o_ref[0, s * LANES : (s + 1) * LANES]
        send_refs[s][LANES:] = r_ref[s, 0]


def back_kernel(
    blocks, apart, q_ref, k_ref, v_ref, o_ref, aug_ref, m_ref, spread_ref, extra_ref, *refs
):
    out_refs, dk_ref, dq_ref = refs[:-2], refs[-2], refs[-1]
    tokens = blocks * LANES
    chunk = row_chunk(tokens)
    count = tokens // chunk
    plain = k_ref[0]
    keys = jnp.concatenate([plain, ones_three((tokens, LANES))], axis=1)
    values = v_ref[0]
    spread = spread_ref[...]

    def scores(i):
        at = chunk_rows(i, chunk)
        s = dot_nt(jnp.concatenate([q_ref[0, at], aug_ref[0, at]], axis=1), keys)
        grad = dot_nn(m_ref[at], spread)
        delta = jnp.sum(grad * o_ref[0, at].astype(F32), axis=1, keepdims=True)
        return s, dot_nt(grad.astype(BF), values), delta

    def products(i, s, dp, delta):
        at = chunk_rows(i, chunk)
        ds = (jnp.exp2(s * (SCALE * LOG2E)) * (dp - delta)).astype(BF)
        dq_ref[at] = (dot_nn(ds, plain) * SCALE).astype(BF)
        return dot_tn(ds, q_ref[0, at])

    if count <= 4:
        ahead = scores(0)
        total = None
        for i in range(count):
            now = ahead
            if i + 1 < count:
                ahead = scores(i + 1)
            part = products(i, *now)
            total = part if total is None else total + part
        dk = (total * SCALE).astype(BF)
    else:
        dk_ref[...] = jnp.zeros(dk_ref.shape, F32)

        def step(i, carry):
            dk_ref[...] += products(i, *scores(i))
            return carry

        lax.fori_loop(0, count, step, 0)
        dk = (dk_ref[...] * SCALE).astype(BF)
    me = lax.axis_index("gen")
    for s in range(blocks):
        at = slice(s * LANES, (s + 1) * LANES)
        out_ref = out_refs[s] if apart else out_refs[0].at[me ^ s]
        out_ref[:LANES] = dq_ref[at]
        out_ref[LANES : 2 * LANES] = dk[at]
        out_ref[2 * LANES : 2 * LANES + FR] = spread[:FR]
        if apart:
            out_ref[2 * LANES + FR :] = extra_ref[...]


def received(blocks, near_refs, far_refs, s):
    near = len(near_refs)
    if s < near:
        return [near_refs[s]]
    return [far_refs[i + s - near] for i in range(0, len(far_refs), blocks - near)]


def value_columns(rows, spread):
    parts = [
        dot_tn(rows[:, at : at + HS], spread[:, at : at + HS]).astype(BF)
        for at in range(0, rows.shape[1], HS)
    ]
    return jnp.concatenate(parts, axis=1) if len(parts) > 1 else parts[0]


def settle_kernel(blocks, lw, first, near, far, *refs):
    near_refs, far_refs, refs = refs[:near], refs[near : near + far], refs[near + far :]
    if first:
        early_ref, latent_ref, rows_ref, dq_ref, dk_ref, dv_ref = refs
    else:
        latent_ref, rows_ref = refs
    me = lax.axis_index("gen")
    for s in range(blocks):
        d = me ^ s
        start = 0
        for ref in received(blocks, near_refs, far_refs, s):
            at = pl.ds(pl.multiple_of(d * lw + start, LANES), ref.shape[1])
            latent_ref[:, at] = ref[:LANES]
            start += ref.shape[1]
        rows = [ref[LANES:] for ref in received(blocks, near_refs, far_refs, s)]
        rows = jnp.concatenate(rows, axis=1) if len(rows) > 1 else rows[0]
        rows_ref[s] = rows[:, first:]
        if first:
            spread = early_ref[d, 2 * LANES :]
            at = pl.ds(pl.multiple_of(d * lw, LANES), first)
            dq_ref[:, at] = early_ref[d, :LANES]
            dk_ref[:, at] = early_ref[d, LANES : 2 * LANES]
            dv_ref[:, at] = value_columns(rows[:, :first], spread)


def finish_kernel(blocks, lw, chunk, *refs):
    late_refs, rows_ref = refs[:blocks], refs[blocks]
    dq_ref, dk_ref, dv_ref, heads_ref, made_ref, sems = refs[-6:]
    me = lax.axis_index("gen")
    last = rows_ref.shape[2]
    per = last // LANES
    copies = []
    for s in range(blocks):
        d = me ^ s
        late = late_refs[s]
        at = pl.ds(pl.multiple_of(d * lw + lw - last, LANES), last)
        made_ref[s] = value_columns(rows_ref[s], late[2 * LANES : 2 * LANES + FR])
        for source, out in (
            (late.at[:LANES], dq_ref),
            (late.at[LANES : 2 * LANES], dk_ref),
            (made_ref.at[s], dv_ref),
        ):
            copies.append(pltpu.make_async_copy(source, out.at[:, at], sems.at[len(copies)]))
            copies[-1].start()
        for piece in range(chunk // LANES):
            row = 2 * LANES + FR + piece // per * NDH
            lane = piece % per * LANES
            at = pl.ds(pl.multiple_of(d * chunk + piece * LANES, LANES), LANES)
            heads_ref[:, at] = late[row : row + NDH, lane : lane + LANES].astype(F32)
    for copy in copies:
        copy.wait()


def exchange(array):
    return lax.all_to_all(array, "gen", split_axis=0, concat_axis=0, tiled=True)


def on_device(
    query_in, key_in, value_in, teacher_w, disc_heads, frame_of_token, head_of_frame, timestep
):
    n = lax.axis_size("gen")
    grp = lax.axis_size("grp")
    me = lax.axis_index("gen")
    tok = query_in.shape[1]
    width = query_in.shape[2]
    tokens = tok * n
    heads = width // HS // n
    lw = heads * HS
    dh = teacher_w.shape[1]
    columns = dh // n
    chunk = -(-columns // LANES) * LANES
    rows = row_chunk(tokens)

    far, near = list(range(n // 2, n)), list(range(1, n // 2))
    half = len(far)

    def columns_for(array, s):
        return lax.dynamic_slice_in_dim(array, (me ^ s) * lw, lw, axis=1)

    def send(array, s):
        return lax.ppermute(array, "gen", [(i, i ^ s) for i in range(n)])

    def query_key(s):
        return jnp.stack([columns_for(query_in[0], s), columns_for(key_in[0], s)])

    qk, v = {0: query_key(0)}, {0: columns_for(value_in[0], 0)}
    blocks = {s: query_key(s) for s in far}
    for s in far:
        qk[s] = send(blocks[s], s)
    most = [qk[s] for s in far[-2:]]
    every = [qk[s] for s in far]
    for s in near:
        behind = [qk[s - 1]] if s > 1 else list(blocks.values())
        qk[s] = send(after(query_key(s), *behind), s)
    for s in near:
        behind = v[s - 1] if s > 1 else qk[s]
        v[s] = send(after(columns_for(value_in[0], s), behind), s)
    for i, s in enumerate(far):
        v[s] = send(after(columns_for(value_in[0], s), *(most if i == half - 1 else every)), s)
    qk, v = [qk[s] for s in range(n)], [v[s] for s in range(n)]

    frames = frame_of_token[0]
    frames = jnp.take(frames.reshape(n, tok), me ^ jnp.arange(n), axis=0).reshape(tokens)
    member = (frames[:, None] == lax.broadcasted_iota(jnp.int32, (tokens, LANES), 1)).astype(BF)
    member_t = (
        frames[None, :] == lax.broadcasted_iota(jnp.int32, (RR, tokens), 0)
    )
    counts = jnp.sum(member_t.astype(F32), axis=1)[:FR]
    member_t = jnp.transpose(
        member_t.astype(BF).reshape(RR, tokens // rows, rows), (1, 0, 2)
    )
    weight = (timestep[0].astype(F32) + 1.0) / NSTEPS
    lane = lax.broadcasted_iota(jnp.int32, (FR, LANES), 1)
    meta = jnp.where(lane == 0, counts[:, None], weight)
    head_ids = jnp.concatenate([head_of_frame[0], jnp.full((FR - FRAMES,), NDH, jnp.int32)])
    picked = (
        head_ids[:, None] == lax.broadcasted_iota(jnp.int32, (FR, NDH), 1)
    ).astype(F32)
    my_heads = lax.dynamic_slice_in_dim(disc_heads, me * columns, columns, axis=1)
    my_heads = jnp.pad(my_heads, ((0, 0), (0, chunk - columns)))
    head_rows = jnp.sum(picked[:, :, None] * my_heads[None], axis=1)
    if chunk == columns:
        w = teacher_w
    else:
        w = jnp.transpose(teacher_w.reshape(lw, n, columns), (1, 0, 2))
        w = jnp.pad(w, ((0, 0), (0, 0), (0, chunk - columns)))

    head_block = pl.BlockSpec((1, tokens, HS), lambda h: (h, 0, 0))
    head_shape = pltpu.HBM((heads, tokens, HS), BF)
    r_block = pl.BlockSpec((n, 1, FR, LANES), lambda h: (0, h, 0, 0))
    square = 2 * tokens * tokens * HS
    in_vmem = pl.BlockSpec(memory_space=pltpu.VMEM)
    anywhere = pl.BlockSpec(memory_space=pl.ANY)
    weights_scratch = [pltpu.VMEM((n, lw, chunk), BF), pltpu.SemaphoreType.DMA((n,))]

    with jax.named_scope("softmax_stats"):
        aug, r, q_rows, k_rows = pl.pallas_call(
            functools.partial(stats_kernel, n),
            grid=(heads,),
            in_specs=[pl.BlockSpec((2, LANES, HS), lambda h: (0, 0, h))] * n
            + [pl.BlockSpec((tokens // rows, RR, rows), lambda h: (0, 0, 0))],
            out_specs=[head_block, r_block, head_block, head_block],
            out_shape=[
                head_shape,
                pltpu.HBM((n, heads, FR, LANES), BF),
                head_shape,
                head_shape,
            ],
            compiler_params=params(tokens),
            cost_estimate=pl.CostEstimate(
                flops=heads * square, bytes_accessed=4 << 20, transcendentals=heads * tokens**2
            ),
        )(*map(hbm, qk), member_t)

    with jax.named_scope("pool_project"):
        part, pooled = pl.pallas_call(
            functools.partial(pool_kernel, n, heads, chunk),
            in_specs=[anywhere] * (n + 1) + [in_vmem, anywhere],
            scratch_shapes=[
                pltpu.VMEM((tokens, lw), BF),
                pltpu.VMEM((n, heads, FR, LANES), BF),
                pltpu.SemaphoreType.DMA((n + 1,)),
            ]
            + weights_scratch,
            out_shape=[
                jax.ShapeDtypeStruct((n, FR, chunk + LANES), BF),
                jax.ShapeDtypeStruct((FR, lw), F32),
            ],
            compiler_params=params(tokens, 0),
        )(*v, hbm(r), meta, hbm(w))

    got = exchange(part)

    split = heads // 2
    parts = [(0, split), (split, heads)] if split else [(0, heads)]

    def output(first, last, behind, before):
        at = pl.BlockSpec((1, tokens, HS), lambda h: (h + first, 0, 0))
        near_at = pl.BlockSpec((LANES + FR, HS), lambda h: (0, h + first))
        far_at = pl.BlockSpec((LANES + FR, HS), lambda h: (0, h))
        shared = [pltpu.HBM((LANES + FR, lw), BF)] * (n - half)
        inputs = list(map(hbm, v + [q_rows, k_rows, aug, after(r, behind)] + before))
        kept = list(range(n - half)) + [n, n + 1]
        with jax.named_scope("attention_output"):
            made = pl.pallas_call(
                functools.partial(output_kernel, n),
                grid=(last - first,),
                in_specs=[pl.BlockSpec((LANES, HS), lambda h: (0, h + first))] * n
                + [at] * 3
                + [pl.BlockSpec((n, 1, FR, LANES), lambda h: (0, h + first, 0, 0))]
                + [anywhere] * len(before),
                out_specs=[near_at] * (n - half) + [far_at] * half + [at] * 2,
                out_shape=shared
                + [pltpu.HBM((LANES + FR, (last - first) * HS), BF)] * half
                + [head_shape] * 2,
                input_output_aliases={n + 4 + i: kept[i] for i in range(len(before))},
                compiler_params=params(tokens),
                cost_estimate=pl.CostEstimate(
                    flops=2 * (last - first) * square,
                    bytes_accessed=(last - first) << 20,
                    transcendentals=(last - first) * tokens**2,
                ),
            )(*inputs)
        return made[: n - half], made[n - half : n], made[n:]

    mixed_near, made, own = output(*parts[0], part, [])
    got = after(got, own[1])
    mixed = [[send(made[i], s) for i, s in enumerate(far)]]

    with jax.named_scope("discriminator"):
        direction, feature, root = pl.pallas_call(
            functools.partial(middle_kernel, n, chunk, width),
            out_shape=[
                jax.ShapeDtypeStruct((n, FR, chunk + LANES), BF),
                jax.ShapeDtypeStruct((FR, chunk), F32),
                jax.ShapeDtypeStruct((FR, LANES), F32),
            ],
            compiler_params=params(tokens, 0),
        )(got, head_rows)

    got_back = exchange(after(direction, mixed[0][0]))
    got_back = after(got_back, *mixed[0][1:])
    if split:
        mixed_near, made, own = output(*parts[1], direction, list(mixed_near) + list(own))
        got_back = after(got_back, own[1])
        rest = made

    with jax.named_scope("pooled_gradient"):
        spread, head_part = pl.pallas_call(
            functools.partial(spread_kernel, n, chunk, width, tokens),
            in_specs=[in_vmem, anywhere] + [in_vmem] * 5,
            scratch_shapes=weights_scratch,
            out_shape=[
                jax.ShapeDtypeStruct((LANES, lw), BF),
                jax.ShapeDtypeStruct((NDH, chunk), F32),
            ],
            compiler_params=params(tokens, 0),
        )(got_back, hbm(w), pooled, meta, root, feature, picked)

    def back(first, last, apart, extra):
        part = (last - first) * HS
        if apart:
            block = (2 * LANES + FR + extra.shape[0], HS)
        else:
            block = (n, 2 * LANES + FR, HS)
        shape = block[:-1] + (part,)
        count = n if apart else 1
        at = pl.BlockSpec((1, tokens, HS), lambda h: (h + first, 0, 0))
        with jax.named_scope("attention_back"):
            return pl.pallas_call(
                functools.partial(back_kernel, n, apart),
                grid=(last - first,),
                in_specs=[at] * 5
                + [
                    pl.BlockSpec((tokens, LANES), lambda h: (0, 0)),
                    pl.BlockSpec((LANES, HS), lambda h: (0, h + first)),
                    pl.BlockSpec((extra.shape[0], HS), lambda h: (0, h)),
                ],
                out_specs=[pl.BlockSpec(block, lambda h: (0,) * (len(block) - 1) + (h,))] * count,
                out_shape=[pltpu.HBM(shape, BF)] * count,
                scratch_shapes=[pltpu.VMEM((tokens, HS), F32), pltpu.VMEM((tokens, HS), BF)],
                compiler_params=params(tokens),
                cost_estimate=pl.CostEstimate(
                    flops=4 * (last - first) * square,
                    bytes_accessed=(last - first) * (2 << 20),
                    transcendentals=(last - first) * tokens**2,
                ),
            )(*map(hbm, [q_rows, k_rows, *own, aug]), member, spread, extra)

    mixed_near = [mixed_near[0]] + [send(mixed_near[s], s) for s in near]
    if split:
        mixed.append([send(after(rest[i], spread), s) for i, s in enumerate(far)])
        spread = after(spread, mixed[1][0], *mixed_near[1:])
    head_sum = head_part
    if grp > 1:
        head_sum = head_sum + lax.ppermute(head_part, "grp", [(i, i ^ 1) for i in range(grp)])
    early = []
    first = split
    if first:
        made = back(0, first, False, jnp.zeros((NDH, first * HS), BF))[0]
        spread, head_sum, made = lax.optimization_barrier((spread, head_sum, made))
        early = [exchange(after(made, mixed[0][-1], *mixed[1]))]

    step = 2
    while step < grp:
        head_sum = head_sum + lax.ppermute(
            head_sum, "grp", [(i, i ^ step) for i in range(grp)]
        )
        step *= 2
    late_width = lw - first * HS
    groups = -(-chunk // late_width)
    extra = jnp.pad(head_sum.astype(BF), ((0, 0), (0, groups * late_width - chunk)))
    extra = jnp.transpose(extra.reshape(NDH, groups, late_width), (1, 0, 2))
    made = back(first, heads, True, extra.reshape(groups * NDH, late_width))
    late = [made[0]] + [send(made[s], s) for s in range(1, n)]

    whole = jax.ShapeDtypeStruct((tok, width), BF)
    far_blocks = [block for blocks in mixed for block in blocks]
    frame_rows = jax.ShapeDtypeStruct((n, FR, late_width), BF)
    with jax.named_scope("settle"):
        latents, frame_rows, *begun = pl.pallas_call(
            functools.partial(settle_kernel, n, lw, first * HS, n - half, len(far_blocks)),
            out_shape=[whole, frame_rows] + ([pltpu.HBM((tok, width), BF)] * 3 if first else []),
            compiler_params=params(tokens, 0),
        )(*mixed_near, *far_blocks, *map(hbm, early))
    late[0] = after(late[0], latents)
    with jax.named_scope("finish"):
        out_query, out_key, out_value, grad_heads = pl.pallas_call(
            functools.partial(finish_kernel, n, lw, chunk),
            in_specs=[in_vmem] * (n + 1) + [anywhere] * len(begun),
            out_specs=[anywhere] * 3 + [in_vmem],
            out_shape=[pltpu.HBM((tok, width), BF)] * 3
            + [jax.ShapeDtypeStruct((NDH, n * chunk), F32)],
            input_output_aliases={n + 1 + i: i for i in range(len(begun))},
            scratch_shapes=[
                pltpu.VMEM((n, LANES, late_width), BF),
                pltpu.SemaphoreType.DMA((3 * n,)),
            ],
            compiler_params=params(tokens, 0),
        )(*late, frame_rows, *map(hbm, begun))
    if chunk != columns:
        grad_heads = grad_heads.reshape(NDH, n, chunk)[:, :, :columns].reshape(NDH, dh)

    return (latents[None], out_query[None], out_key[None], out_value[None], grad_heads)


def solution(mesh):
    return jax.shard_map(
        on_device,
        mesh=mesh,
        in_specs=(
            P("grp", "gen", None),
            P("grp", "gen", None),
            P("grp", "gen", None),
            P("gen", None),
            P(),
            P("grp", None),
            P("grp", None),
            P("grp"),
        ),
        out_specs=(
            P("grp", "gen", None),
            P("grp", "gen", None),
            P("grp", "gen", None),
            P("grp", "gen", None),
            P(),
        ),
        check_vma=False,
    )
```
